512 devices in a mesh: replica: 16 (over z_hi, y, core), fsdp: 32 (over x, z_lo).
Axes of the slice: x: 4, y: 4, z: 16 (z_hi: 2, z_lo: 8; z = z_hi * 8 + z_lo), core: 2. Of those that a mesh axis runs over, the one named last changes fastest.
Arguments:
- local_weights: bfloat16 [16, 2048, 512], P('replica', 'fsdp'), may hold values from -0.125 to 0.125
- global_weights: bfloat16 [2048, 512], P('fsdp'), may hold values from -0.125 to 0.125
- momentum: float32 [2048, 512], P('fsdp', 'replica'), may hold values from -0.12 to 0.12
- activations: bfloat16 [16, 8192, 2048], P('replica', 'fsdp'), may hold values from -6 to 6
- kv_cotangent: bfloat16 [16, 8192, 512], P('replica', 'fsdp'), may hold values from -6 to 6
Outputs:
- kv_rows: bfloat16 [16, 8192, 512], P('replica', 'fsdp')
- input_grad: bfloat16 [16, 8192, 2048], P('replica', 'fsdp')
- weight_grad: bfloat16 [16, 2048, 512], P('replica', 'fsdp')
- new_global: bfloat16 [2048, 512], P('fsdp')
- new_momentum: float32 [2048, 512], P('fsdp', 'replica')
The draws below stay inside these ranges and needn't reach their ends.
All inputs are finite; a program needn't handle non-finite values. Where the reference program divides by a largest or mean magnitude, that divisor is 1e-20 or more.
Results may differ from the reference program's by a relative error of at most 0.0038.
Values may be sent and summed in bfloat16 or wider, within the bound.
A program may use at most 64 MiB of HBM per device.

```python
import jax
import jax.numpy as jnp
from jax import lax

D = 2048
KV = 512
BLOCK = 64
TOKENS = 8192
N_REPLICA = 16


def raised(drawn, rng, source, target, shards_of, factor):
    owner, partner = [(jnp.arange(drawn.shape[dim]) // (drawn.shape[dim] // shards_of)).reshape([-1 if axis == dim else 1 for axis in range(drawn.ndim)]) for dim in (source, target)]
    chosen = jax.random.permutation(rng, shards_of)[partner]
    strong = (owner == chosen) | (owner == (partner + shards_of // 2) % shards_of)
    return jnp.where(strong, factor * drawn, drawn)


def block_levels(key, shape, shards, smallest, largest):
    def one(position, parts):
        heights = jax.random.uniform(jax.random.fold_in(jax.random.fold_in(key, 6), position), (parts,), jnp.float32, smallest / len(shards), largest / len(shards))
        return jnp.repeat(jnp.exp(heights), shape[position] // parts).reshape((-1,) + (1,) * (len(shape) - position - 1))

    factor_of = one(*shards[0])
    for cut in shards[1:]:
        factor_of = factor_of * one(*cut)
    return factor_of


def bell_draw(rng, dims, scale, limit, split=(), held_as=jnp.bfloat16):
    level = block_levels(rng, dims, split, -0.22, 0.18) if split else 1.0
    entries = jax.random.normal(rng, dims, jnp.float32) * scale * level
    return jnp.minimum(jnp.maximum(entries, -limit), limit).astype(held_as)


def gaussian_with(rng, dims, deviation, limit, split, heavy, dtype=jnp.bfloat16):
    entries = deviation * jax.random.normal(rng, dims, jnp.float32)
    if split:
        entries = entries * block_levels(rng, dims, split, -0.22, 0.18)
    return jnp.clip(raised(entries, jax.random.fold_in(rng, 3), *heavy), -limit, limit).astype(dtype)


def setup_inputs(seed: int = 0) -> dict:
    splits = jax.random.split(jax.random.key(seed), 6)
    local_weights = bell_draw(splits[0], (N_REPLICA, D, KV), D ** -0.5, 0.125, ((0, 16), (1, 32)))
    global_weights = bell_draw(splits[1], (D, KV), D ** -0.5, 0.125, ((0, 32),))
    momentum = bell_draw(splits[2], (D, KV), 0.02, 0.12, ((0, 32), (1, 16)), jnp.float32)
    activations = gaussian_with(splits[3], (N_REPLICA, TOKENS, D), 1.0, 6.0, ((0, 16), (1, 32)), (1, 2, 32, 2.75))
    kv_cotangent = bell_draw(splits[4], (N_REPLICA, TOKENS, KV), 1.0, 6.0, ((0, 16), (1, 32)))
    return {"local_weights": local_weights, "global_weights": global_weights, "momentum": momentum, "activations": activations, "kv_cotangent": kv_cotangent}


outer_rate = 0.7
outer_momentum = 0.9
scale_epsilon = 1e-6


def reference(local_weights, global_weights, momentum, activations, kv_cotangent):
    token_weight = 1.0 / TOKENS

    def inner_step(items):
        weights_one, inputs_one, cotangent_one = items
        kv_one = jnp.dot(inputs_one, weights_one, preferred_element_type=jnp.float32).astype(jnp.bfloat16)
        grad_in = jnp.dot(cotangent_one, weights_one.T, preferred_element_type=jnp.float32).astype(jnp.bfloat16)
        summed = jnp.dot(inputs_one.T, cotangent_one, preferred_element_type=jnp.float32) * token_weight
        return kv_one, grad_in, summed.astype(jnp.bfloat16)

    kv_rows, input_grad, weight_grad = lax.map(inner_step, (local_weights, activations, kv_cotangent))

    drift = global_weights.astype(jnp.float32)[None] - local_weights.astype(jnp.float32)
    drift_blocks = drift.reshape(N_REPLICA, D, KV // BLOCK, BLOCK)
    block_scale = (jnp.max(jnp.abs(drift_blocks), axis=3) + scale_epsilon).astype(jnp.bfloat16)
    block_scale = lax.optimization_barrier(block_scale)
    quantized = (drift_blocks / block_scale.astype(jnp.float32)[..., None]).astype(jnp.bfloat16)
    quantized = lax.optimization_barrier(quantized)
    dequantized = quantized.astype(jnp.float32) * block_scale.astype(jnp.float32)[..., None]
    mean_grad = jnp.sum(dequantized, axis=0).reshape(D, KV) / N_REPLICA
    new_momentum = outer_momentum * momentum + mean_grad
    new_global = (global_weights.astype(jnp.float32) - outer_rate * (mean_grad + outer_momentum * new_momentum)).astype(jnp.bfloat16)
    return kv_rows, input_grad, weight_grad, new_global, new_momentum
```

```python
import functools

import jax
import jax.numpy as jnp
from jax import lax
from jax.experimental import pallas as pl
from jax.experimental.pallas import tpu as pltpu
from jax.sharding import PartitionSpec as P

MESH = pl.DeviceIdType.MESH
BLOCK = 64
NX = 4
NZ = 8
NB = 8
ROWS = 64
KV = 512
D = 2048
TOK = 256
HALF = ROWS // 2
COL = NZ * ROWS

outer_rate = 0.7
outer_momentum = 0.9
scale_epsilon = 1e-06

F32 = jnp.float32
BF16 = jnp.bfloat16


def kernel(
    l_hbm, g_hbm, m_hbm, a_hbm, c_hbm,
    kv_hbm, ig_hbm, wg_hbm, ng_hbm, nm_hbm,
    a, ct, w, g, mom, kv, ig, wg, ng, nm,
    s1s, s1r, s2s, s2r, keep, xs, zs, zr, oms, omr, ps, pr, ngs, ngr,
    lsem, osem,
    s1ss, s1rs, s2ss, s2rs, zss, zrs, gzs, gzr, gxs, gxr, ghs, ghr, oas, oar, pss, prs, ogs, ogr,
):
    r = lax.axis_index("replica")
    f = lax.axis_index("fsdp")
    x = f // NZ
    j = f % NZ
    zh = r // NB
    b = r % NB

    def fs(xx, jj):
        return (r, (xx + NX) % NX * NZ + jj)

    def rowof(xx, q):
        return pl.ds(pl.multiple_of(((xx + NX) % NX * NZ + q) * ROWS, ROWS), ROWS)

    def halfof(xx, q, h):
        return pl.ds(pl.multiple_of(((xx + NX) % NX * NZ + q) * ROWS + h * HALF, HALF), HALF)

    def rcopy(src, dst, ss, rs, device):
        return pltpu.make_async_remote_copy(
            src_ref=src, dst_ref=dst, send_sem=ss, recv_sem=rs, device_id=device, device_id_type=MESH
        )

    in_a = pltpu.make_async_copy(a_hbm, a, lsem.at[0])
    in_c = pltpu.make_async_copy(c_hbm, ct, lsem.at[1])
    in_w = pltpu.make_async_copy(l_hbm, w.at[rowof(x, j)], lsem.at[2])
    in_g = pltpu.make_async_copy(g_hbm, g, lsem.at[3])
    in_m = pltpu.make_async_copy(m_hbm, mom, lsem.at[4])
    for cp in (in_a, in_c, in_w, in_g, in_m):
        cp.start()

    zpos = zh * NZ + j
    barrier = pltpu.get_barrier_semaphore()
    friends = [fs(x + 1, j), fs(x - 1, j)]
    for dz in (1, 15):
        zz = (zpos + dz) % 16
        friends.append((zz // NZ * NB + b, x * NZ + zz % NZ))
    for o in range(1, NB):
        friends.append((zh * NB + (b + o) % NB, f))
    friends.append(((r + NB) % 16, f))
    for dev in friends:
        pl.semaphore_signal(barrier, inc=1, device_id=dev, device_id_type=MESH)

    def xdev(d):
        return fs(x + 1, j) if d == 0 else fs(x - 1, j)

    def c1(d, p):
        return rcopy(s1s.at[d, p], s1r.at[d, p], s1ss.at[d, p], s1rs.at[d, p], xdev(d))

    def c2(d, p):
        return rcopy(s2s.at[d, p], s2r.at[d, p], s2ss.at[d, p], s2rs.at[d, p], xdev(d))

    def cz(d, p, h):
        rows = pl.ds(h * HALF, HALF)
        return rcopy(
            zs.at[d, p, rows], zr.at[d, p, rows], zss.at[d, h, p], zrs.at[d, h, p],
            fs(x, j + 1 if d == 0 else j - 1),
        )

    def cgz(d, q):
        return rcopy(
            w.at[rowof(x, q)], w.at[rowof(x, q)], gzs.at[d, q], gzr.at[d, q],
            fs(x, j + 1 if d == 0 else j - 1),
        )

    def cgx(d, q):
        return rcopy(w.at[rowof(x, q)], w.at[rowof(x, q)], gxs.at[d, q], gxr.at[d, q], xdev(d))

    def wgx(d, q):
        src = x - 1 if d == 0 else x + 1
        return rcopy(w.at[rowof(src, q)], w.at[rowof(src, q)], gxs.at[d, q], gxr.at[d, q], xdev(d))

    def cgh(d, q):
        src = x - 1 if d == 0 else x + 1
        return rcopy(
            w.at[halfof(src, q, d)], w.at[halfof(src, q, d)], ghs.at[d, q], ghr.at[d, q], xdev(d)
        )

    def wgh(d, q):
        return rcopy(
            w.at[halfof(x + 2, q, d)], w.at[halfof(x + 2, q, d)], ghs.at[d, q], ghr.at[d, q], xdev(d)
        )

    def coa(o):
        to = (b + o) % NB
        return rcopy(oms.at[to], omr.at[o], oas.at[o], oar.at[o], (zh * NB + to, f))

    def cog(o):
        to = (b + o) % NB
        return rcopy(ngs, ngr.at[o], ogs.at[o], ogr.at[o], (zh * NB + to, f))

    def cpartner():
        return rcopy(ps, pr, pss, prs, ((r + NB) % 16, f))

    in_a.wait()
    in_c.wait()

    def partial_block(xx):
        start = pl.multiple_of((xx + NX) % NX * COL, COL)
        return lax.dot_general(
            a[:, pl.ds(start, COL)], ct[...], (((0,), (0,)), ((), ())), preferred_element_type=F32
        )

    far = partial_block(x + 2).astype(BF16).reshape(NZ, ROWS, KV)
    s1s[0, :, 0:HALF, :] = far[:, :HALF, :]
    s1s[1, :, 0:HALF, :] = far[:, HALF:, :]
    right = partial_block(x + 1).reshape(NZ, ROWS, KV)
    s1s[0, :, HALF:, :] = right[:, HALF:, :].astype(BF16)
    keep[0] = right[:, :HALF, :]
    left = partial_block(x - 1).reshape(NZ, ROWS, KV)
    s1s[1, :, HALF:, :] = left[:, :HALF, :].astype(BF16)
    keep[1] = left[:, HALF:, :]

    pl.semaphore_wait(barrier, len(friends))

    in_w.wait()

    def z_forward(k):
        @pl.when((j - k >= 0) & (j < NZ - 1))
        def _():
            cgz(0, j - k).start()

        @pl.when((j + k < NZ) & (j > 0))
        def _():
            cgz(1, j + k).start()

    def z_arrive(k):
        @pl.when(j - k >= 0)
        def _():
            cgz(0, j - k).wait_recv()

        @pl.when(j + k < NZ)
        def _():
            cgz(1, j + k).wait_recv()

    def z_gather(k):
        z_arrive(k)
        if k < NZ - 1:
            z_forward(k)

    def pair(i):
        return (NZ - 1 - i, i)

    def start1(i):
        for p in pair(i):
            for d in range(2):
                c1(d, p).start()

    def relay(i):
        for p in pair(i):
            for d in range(2):
                c1(d, p).wait_recv()
                s2s[d, p] = (keep[d, p] + s1r[d, p, 0:HALF].astype(F32)).astype(BF16)
                c2(d, p).start()

    def settle(i):
        for p in pair(i):
            c2(0, p).wait_recv()
            xs[p, 0:HALF] += s2r[0, p].astype(F32) + s1r[1, p, HALF:].astype(F32)
            c2(1, p).wait_recv()
            xs[p, HALF:] += s2r[1, p].astype(F32) + s1r[0, p, HALF:].astype(F32)

    def z_step(s):
        pa = NZ - 1 - s + j
        pb = s - (NZ - 1) + j
        for h in range(2):
            rows = pl.ds(h * HALF, HALF)

            @pl.when(j <= s)
            def _():
                @pl.when(j == 0)
                def _():
                    zs[0, pa, rows] = xs[pa, rows]

                @pl.when(j > 0)
                def _():
                    cz(0, pa, h).wait_recv()
                    zs[0, pa, rows] = xs[pa, rows] + zr[0, pa, rows]

                cz(0, pa, h).start()

            @pl.when(pb >= 0)
            def _():
                @pl.when(j == NZ - 1)
                def _():
                    zs[1, pb, rows] = xs[pb, rows]

                @pl.when(j < NZ - 1)
                def _():
                    cz(1, pb, h).wait_recv()
                    zs[1, pb, rows] = xs[pb, rows] + zr[1, pb, rows]

                cz(1, pb, h).start()

    def z_final():
        for h in range(2):
            rows = pl.ds(h * HALF, HALF)

            @pl.when(j > 0)
            def _():
                cz(0, j, h).wait_recv()
                xs[j, rows] += zr[0, j, rows]

            @pl.when(j < NZ - 1)
            def _():
                cz(1, j, h).wait_recv()
                xs[j, rows] += zr[1, j, rows]

    def chunk(n):
        m = jnp.minimum(j, NZ - 1 - j)
        near = j - (n + 1) // 2 if n % 2 else j + n // 2
        rest = jnp.where(j < NZ // 2, n, NZ - 1 - n)
        return jnp.where(n <= 2 * m, near, rest)

    def x_send(n):
        for d in range(2):
            cgx(d, chunk(n)).start()

    def x_relay(n):
        q = chunk(n)
        for d in range(2):
            wgx(d, q).wait_recv()
            cgh(d, q).start()

    z_forward(0)
    start1(0)
    start1(1)

    xs[...] = partial_block(x).reshape(NZ, ROWS, KV)

    in_g.wait()
    in_m.wait()
    drift = g[...].astype(F32) - w[rowof(x, j), :].astype(F32)
    codes, scales = [], []
    for k in range(KV // BLOCK):
        blk = drift[:, k * BLOCK : (k + 1) * BLOCK]
        scale = (jnp.max(jnp.abs(blk), axis=1, keepdims=True) + scale_epsilon).astype(BF16)
        codes.append((blk / scale.astype(F32)).astype(BF16))
        scales.append(jnp.broadcast_to(scale.astype(F32), (ROWS, BLOCK // 2)).astype(BF16))
    hb = BLOCK // 2
    for t in range(NB):
        yy, cc = t // 2, t % 2
        cut = slice(cc * hb, cc * hb + hb)
        oms[t] = jnp.concatenate(
            [codes[yy][:, cut], codes[yy + 4][:, cut], scales[yy], scales[yy + 4]], axis=1
        )
    for o in range(1, NB):
        coa(o).start()

    def outer_sum():
        for o in range(1, NB):
            coa(o).wait_recv()
        mine = oms[b].astype(F32)
        total = mine[:, :BLOCK] * mine[:, BLOCK:]
        for o in range(1, NB):
            got = omr[o].astype(F32)
            total += got[:, :BLOCK] * got[:, BLOCK:]
        ps[0:32] = jnp.concatenate([total[:32], total[32:]], axis=1)
        m = mom[...]
        ps[32:48] = jnp.concatenate([m[:16], m[16:32], m[32:48], m[48:]], axis=1)
        cpartner().start()

    def outer_update():
        cpartner().wait_recv()
        both = ps[0:32] + pr[0:32]
        mean = jnp.concatenate([both[:, :BLOCK], both[:, BLOCK:]], axis=0) / 16.0
        pm = pr[32:48]
        theirs = jnp.concatenate([pm[:, 0:32], pm[:, 32:64], pm[:, 64:96], pm[:, 96:]], axis=0)
        ours = mom[...]
        low = zh == 0
        m64 = jnp.concatenate([jnp.where(low, ours, theirs), jnp.where(low, theirs, ours)], axis=1)
        old = jnp.zeros((ROWS, BLOCK), F32)
        for t in range(NB):
            yy, cc = t // 2, t % 2
            lo = yy * BLOCK + cc * hb
            pick = jnp.concatenate([g[:, lo : lo + hb], g[:, 256 + lo : 256 + lo + hb]], axis=1)
            old = jnp.where(b == t, pick.astype(F32), old)
        new_m = outer_momentum * m64 + mean
        share = (old - outer_rate * (mean + outer_momentum * new_m)).astype(BF16)
        nm[...] = jnp.where(low, new_m[:, :hb], new_m[:, hb:])
        ngs[...] = jnp.concatenate([share, share], axis=1)
        for o in range(1, NB):
            cog(o).start()

    def outer_collect():
        for o in range(1, NB):
            cog(o).wait_recv()
        ngr[0] = ngs[...]
        for t in range(NB):
            yy, cc = t // 2, t % 2
            lo = yy * BLOCK + cc * hb
            got = ngr[(b - t + NB) % NB]
            ng[:, lo : lo + hb] = got[:, :hb]
            ng[:, 256 + lo : 256 + lo + hb] = got[:, hb:BLOCK]

    def use_column(xx, first):
        start = pl.multiple_of((xx + NX) % NX * COL, COL)
        wc = w[pl.ds(start, COL), :]
        part = jnp.dot(a[:, pl.ds(start, COL)], wc, preferred_element_type=F32)
        if first:
            kv[...] = part
        else:
            kv[...] += part
        ig[:, pl.ds(start, COL)] = lax.dot_general(
            ct[...], wc, (((1,), (1,)), ((), ())), preferred_element_type=F32
        ).astype(BF16)

    relay(0)
    start1(2)
    z_gather(1)
    relay(1)
    start1(3)
    settle(0)
    z_step(0)
    z_gather(2)
    outer_sum()
    z_gather(3)
    relay(2)
    settle(1)
    z_step(1)
    z_gather(4)
    z_gather(5)
    relay(3)
    x_send(0)
    settle(2)
    z_step(2)
    x_send(1)
    x_send(2)
    x_send(3)
    z_gather(6)
    settle(3)
    z_step(3)
    outer_update()
    x_send(4)
    x_send(5)
    z_gather(7)
    x_send(6)
    x_send(7)
    x_relay(0)
    x_relay(1)
    z_step(4)
    x_relay(2)
    x_relay(3)
    use_column(x, True)
    z_step(5)
    x_relay(4)
    x_relay(5)
    outer_collect()
    out_ng = pltpu.make_async_copy(ng, ng_hbm, osem.at[0])
    out_nm = pltpu.make_async_copy(nm, nm_hbm, osem.at[1])
    out_ng.start()
    out_nm.start()
    z_step(6)
    x_relay(6)
    x_relay(7)
    z_final()
    wg[...] = (xs[j] * (1.0 / (TOK * NX * NZ))).astype(BF16)
    out_wg = pltpu.make_async_copy(wg, wg_hbm, osem.at[2])
    out_wg.start()
    use_column(x + 1, False)
    use_column(x - 1, False)
    for n in range(NZ):
        for d in range(2):
            wgh(d, chunk(n)).wait_recv()
    use_column(x + 2, False)
    out_ig = pltpu.make_async_copy(ig, ig_hbm, osem.at[3])
    out_ig.start()
    a[:, 0:KV] = kv[...].astype(BF16)
    out_kv = pltpu.make_async_copy(a.at[:, 0:KV], kv_hbm, osem.at[4])
    out_kv.start()

    for p in range(NZ):
        for d in range(2):
            c1(d, p).wait_send()
            c2(d, p).wait_send()
            cgx(d, p).wait_send()
            cgh(d, p).wait_send()
        for h in range(2):
            @pl.when(p > j)
            def _():
                cz(0, p, h).wait_send()

            @pl.when(p < j)
            def _():
                cz(1, p, h).wait_send()

        @pl.when((p <= j) & (j < NZ - 1))
        def _():
            cgz(0, p).wait_send()

        @pl.when((p >= j) & (j > 0))
        def _():
            cgz(1, p).wait_send()

    for o in range(1, NB):
        coa(o).wait_send()
        cog(o).wait_send()
    cpartner().wait_send()
    for cp in (out_ng, out_nm, out_wg, out_ig, out_kv):
        cp.wait()


def per_device(local_weights, global_weights, momentum, activations, kv_cotangent):
    dma = pltpu.SemaphoreType.DMA
    hbm = pl.BlockSpec(memory_space=pl.ANY)
    outs = pl.pallas_call(
        kernel,
        name="joined_step",
        out_shape=(
            jax.ShapeDtypeStruct((TOK, KV), BF16),
            jax.ShapeDtypeStruct((TOK, D), BF16),
            jax.ShapeDtypeStruct((ROWS, KV), BF16),
            jax.ShapeDtypeStruct((ROWS, KV), BF16),
            jax.ShapeDtypeStruct((ROWS, 32), F32),
        ),
        in_specs=[hbm] * 5,
        out_specs=[hbm] * 5,
        scratch_shapes=[
            pltpu.VMEM((TOK, D), BF16),
            pltpu.VMEM((TOK, KV), BF16),
            pltpu.VMEM((D, KV), BF16),
            pltpu.VMEM((ROWS, KV), BF16),
            pltpu.VMEM((ROWS, 32), F32),
            pltpu.VMEM((TOK, KV), F32),
            pltpu.VMEM((TOK, D), BF16),
            pltpu.VMEM((ROWS, KV), BF16),
            pltpu.VMEM((ROWS, KV), BF16),
            pltpu.VMEM((ROWS, 32), F32),
            pltpu.VMEM((2, NZ, ROWS, KV), BF16),
            pltpu.VMEM((2, NZ, ROWS, KV), BF16),
            pltpu.VMEM((2, NZ, HALF, KV), BF16),
            pltpu.VMEM((2, NZ, HALF, KV), BF16),
            pltpu.VMEM((2, NZ, HALF, KV), F32),
            pltpu.VMEM((NZ, ROWS, KV), F32),
            pltpu.VMEM((2, NZ, ROWS, KV), F32),
            pltpu.VMEM((2, NZ, ROWS, KV), F32),
            pltpu.VMEM((NB, ROWS, 128), BF16),
            pltpu.VMEM((NB, ROWS, 128), BF16),
            pltpu.VMEM((48, 128), F32),
            pltpu.VMEM((48, 128), F32),
            pltpu.VMEM((ROWS, 128), BF16),
            pltpu.VMEM((NB, ROWS, 128), BF16),
            dma((5,)),
            dma((5,)),
            dma((2, NZ)), dma((2, NZ)),
            dma((2, NZ)), dma((2, NZ)),
            dma((2, 2, NZ)), dma((2, 2, NZ)),
            dma((2, NZ)), dma((2, NZ)),
            dma((2, NZ)), dma((2, NZ)),
            dma((2, NZ)), dma((2, NZ)),
            dma((NB,)), dma((NB,)),
            dma(()), dma(()),
            dma((NB,)), dma((NB,)),
        ],
        compiler_params=pltpu.CompilerParams(
            collective_id=0, has_side_effects=True, vmem_limit_bytes=40 * 2**20
        ),
        cost_estimate=pl.CostEstimate(
            flops=6 * TOK * D * KV, bytes_accessed=6 * 2**20, transcendentals=0
        ),
    )(local_weights[0], global_weights, momentum, activations[0], kv_cotangent[0])
    kv, ig, wg, ng, nm = outs
    return kv[None], ig[None], wg[None], ng, nm


def solution(mesh):
    placed = (
        P("replica", "fsdp", None),
        P("fsdp", None),
        P("fsdp", "replica"),
        P("replica", "fsdp", None),
        P("replica", "fsdp", None),
    )
    return jax.shard_map(
        per_device,
        mesh=mesh,
        in_specs=placed,
        out_specs=(
            P("replica", "fsdp", None),
            P("replica", "fsdp", None),
            P("replica", "fsdp", None),
            P("fsdp", None),
            P("fsdp", "replica"),
        ),
        check_vma=False,
    )
```

```python
import functools

import jax
import jax.numpy as jnp
from jax import lax
from jax.experimental import pallas as pl
from jax.experimental.pallas import tpu as pltpu
from jax.sharding import PartitionSpec as P

MESH = pl.DeviceIdType.MESH
BLOCK = 64
KERNEL_VMEM = 40 * 2**20
NX = 4
NZ = 8
NB = 8
ROWS = 64
KV = 512
D = 2048
TOK = 256
HALF = ROWS // 2
NLINE = 16
COL = NZ * ROWS

outer_rate = 0.7
outer_momentum = 0.9
scale_epsilon = 1e-06

F32 = jnp.float32
BF16 = jnp.bfloat16


def kernel(
    l_hbm, g_hbm, m_hbm, a_hbm, c_hbm,
    kv_hbm, ig_hbm, wg_hbm, ng_hbm, nm_hbm,
    a, ct, w, g, mom, kv, kvb, ig, wg, ng, nm,
    s1s, s1r, s2s, s2r, keep, xs, z1s, z1r, z2s, z2r, z3s, z3r, oms, omr, ps, pr, ngs, ngr,
    lsem, osem, near, next2, next4,
    tss, trs, oss, ors, s2ss, s2rs, z1ss, z1rs, z2ss, z2rs, z3ss, z3rs,
    gzs, gzr, gxs, gxr, ghs, ghr, oas, oar, pss, prs, ogs, ogr,
):
    r = lax.axis_index("replica")
    f = lax.axis_index("fsdp")
    x = f // NZ
    j = f % NZ
    zh = r // NB
    b = r % NB
    zpos = zh * NZ + j
    bits = (j % 2, j // 2 % 2, j // 4)

    def away(t):
        p = j
        for k in range(3):
            if t >> k & 1:
                p = p + (1 << k) * (1 - 2 * bits[k])
        return p

    def fs(xx, jj):
        return (r, (xx + NX) % NX * NZ + jj)

    def line(zz):
        return (zz // NZ * NB + b, x * NZ + zz % NZ)

    def rowof(xx, q):
        return pl.ds(pl.multiple_of(((xx + NX) % NX * NZ + q) * ROWS, ROWS), ROWS)

    def halfof(xx, q, h):
        return pl.ds(pl.multiple_of(((xx + NX) % NX * NZ + q) * ROWS + h * HALF, HALF), HALF)

    def rcopy(src, dst, ss, rs, device):
        return pltpu.make_async_remote_copy(
            src_ref=src, dst_ref=dst, send_sem=ss, recv_sem=rs, device_id=device, device_id_type=MESH
        )

    def signal(sem, device):
        pl.semaphore_signal(sem, inc=1, device_id=device, device_id_type=MESH)

    barrier = pltpu.get_barrier_semaphore()
    friends = [fs(x + 1, j), fs(x - 1, j)]
    for o in range(1, NB):
        friends.append((zh * NB + (b + o) % NB, f))
    for dev in friends:
        signal(barrier, dev)

    @pl.when(zpos > 0)
    def _():
        signal(barrier, line(zpos - 1))

    @pl.when(zpos < NLINE - 1)
    def _():
        signal(barrier, line(zpos + 1))

    in_a = pltpu.make_async_copy(a_hbm, a, lsem.at[0])
    in_c = pltpu.make_async_copy(c_hbm, ct, lsem.at[1])
    in_w = pltpu.make_async_copy(l_hbm, w.at[rowof(x, j)], lsem.at[2])
    in_g = pltpu.make_async_copy(g_hbm, g, lsem.at[3])
    in_m = pltpu.make_async_copy(m_hbm, mom, lsem.at[4])
    for cp in (in_c, in_a, in_w, in_g, in_m):
        cp.start()

    def tell1():
        @pl.when(zpos > 0)
        def _():
            signal(near.at[1], line(zpos - 1))

        @pl.when(zpos < NLINE - 1)
        def _():
            signal(near.at[0], line(zpos + 1))

    def hear1():
        @pl.when(zpos > 0)
        def _():
            pl.semaphore_wait(near.at[0], 1)

        @pl.when(zpos < NLINE - 1)
        def _():
            pl.semaphore_wait(near.at[1], 1)

    def tell2():
        @pl.when(zpos > 1)
        def _():
            signal(next2.at[1], line(zpos - 2))

        @pl.when(zpos < NLINE - 2)
        def _():
            signal(next2.at[0], line(zpos + 2))

    def hear2(inner):
        low = j < NZ // 2 if inner else j >= NZ // 2
        high = j >= NZ // 2 if inner else j < NZ // 2

        @pl.when(high & (zpos > 1))
        def _():
            pl.semaphore_wait(next2.at[0], 1)

        @pl.when(low & (zpos < NLINE - 2))
        def _():
            pl.semaphore_wait(next2.at[1], 1)

    def tell4():
        @pl.when((zpos >= 4) & (zpos < NZ + 4))
        def _():
            signal(next4, line(zpos - 4))

        @pl.when((zpos >= NZ - 4) & (zpos < NLINE - 4))
        def _():
            signal(next4, line(zpos + 4))

    def hear4():
        pl.semaphore_wait(next4, 1)

    def xdev(d):
        return fs(x + 1, j) if d == 0 else fs(x - 1, j)

    top, bottom = slice(0, HALF), slice(HALF, ROWS)

    def c_transit(d, p):
        return rcopy(s1s.at[d, p, top], s1r.at[d, p, top], tss.at[d, p], trs.at[d, p], xdev(d))

    def c_own(d, p):
        return rcopy(s1s.at[d, p, bottom], s1r.at[d, p, bottom], oss.at[d, p], ors.at[d, p], xdev(d))

    def c_sum(d, p):
        return rcopy(s2s.at[d, p], s2r.at[d, p], s2ss.at[d, p], s2rs.at[d, p], xdev(d))

    def cz1(t):
        return rcopy(z1s.at[t // 2], z1r.at[t // 2], z1ss.at[t // 2], z1rs.at[t // 2], fs(x, away(1)))

    def cz2(t):
        return rcopy(z2s.at[t // 4], z2r.at[t // 4], z2ss.at[t // 4], z2rs.at[t // 4], fs(x, away(2)))

    def cz3():
        return rcopy(z3s, z3r, z3ss, z3rs, fs(x, away(4)))

    def cgz(t):
        k = t & -t
        rows = rowof(x, away(t - k))
        return rcopy(w.at[rows], w.at[rows], gzs.at[t], gzr.at[t], fs(x, away(k)))

    def wgz(t):
        rows = rowof(x, away(t))
        return rcopy(w.at[rows], w.at[rows], gzs.at[t], gzr.at[t], fs(x, away(t & -t)))

    def cgx(d, q):
        return rcopy(w.at[rowof(x, q)], w.at[rowof(x, q)], gxs.at[d, q], gxr.at[d, q], xdev(d))

    def wgx(d, q):
        src = x - 1 if d == 0 else x + 1
        return rcopy(w.at[rowof(src, q)], w.at[rowof(src, q)], gxs.at[d, q], gxr.at[d, q], xdev(d))

    def cgh(d, q):
        src = x - 1 if d == 0 else x + 1
        return rcopy(
            w.at[halfof(src, q, d)], w.at[halfof(src, q, d)], ghs.at[d, q], ghr.at[d, q], xdev(d)
        )

    def wgh(d, q):
        return rcopy(
            w.at[halfof(x + 2, q, d)], w.at[halfof(x + 2, q, d)], ghs.at[d, q], ghr.at[d, q], xdev(d)
        )

    def coa(o):
        to = (b + o) % NB
        return rcopy(oms.at[to], omr.at[o], oas.at[o], oar.at[o], (zh * NB + to, f))

    def cog(o):
        to = (b + o) % NB
        return rcopy(ngs, ngr.at[o], ogs.at[o], ogr.at[o], (zh * NB + to, f))

    def cpartner():
        return rcopy(ps, pr, pss, prs, ((r + NB) % (2 * NB), f))

    def partial_block(xx):
        start = pl.multiple_of((xx + NX) % NX * COL, COL)
        return lax.dot_general(
            a[:, pl.ds(start, COL)], ct[...], (((0,), (0,)), ((), ())), preferred_element_type=F32
        ).reshape(NZ, ROWS, KV)

    in_c.wait()
    in_a.wait()
    far = partial_block(x + 2).astype(BF16)
    s1s[0, :, 0:HALF, :] = far[:, :HALF, :]
    s1s[1, :, 0:HALF, :] = far[:, HALF:, :]
    in_w.wait()
    pl.semaphore_wait(barrier, len(friends) + jnp.minimum(zpos, 1) + jnp.minimum(NLINE - 1 - zpos, 1))
    tell1()
    order = (7, 6, 5, 4, 3, 2, 1, 0)
    for t in order:
        for d in range(2):
            c_transit(d, away(t)).start()
    cgz(1).start()

    right = partial_block(x + 1)
    s1s[0, :, HALF:, :] = right[:, HALF:, :].astype(BF16)
    keep[0] = right[:, :HALF, :]
    left = partial_block(x - 1)
    s1s[1, :, HALF:, :] = left[:, :HALF, :].astype(BF16)
    keep[1] = left[:, HALF:, :]

    def relay(t):
        p = away(t)
        for d in range(2):
            c_own(d, p).start()
            c_transit(d, p).wait_recv()
            s2s[d, p] = (keep[d, p] + s1r[d, p, top].astype(F32)).astype(BF16)
            c_sum(d, p).start()

    def settle(t):
        p = away(t)
        for d in range(2):
            c_own(d, p).wait_recv()
        for d in range(2):
            c_sum(d, p).wait_recv()
        xs[p, top] += s2r[0, p].astype(F32) + s1r[1, p, bottom].astype(F32)
        xs[p, bottom] += s2r[1, p].astype(F32) + s1r[0, p, bottom].astype(F32)
        if t % 2:
            z1s[t // 2] = xs[p].astype(BF16)
            cz1(t).start()

    def round1(t):
        cz1(t + 1).wait_recv()
        xs[away(t)] += z1r[t // 2].astype(F32)
        if t % 4 == 2:
            z2s[t // 4] = xs[away(t)].astype(BF16)
            cz2(t).start()

    def round2(t):
        cz2(t + 2).wait_recv()
        xs[away(t)] += z2r[t // 4].astype(F32)
        if t == 4:
            z3s[...] = xs[away(t)]
            cz3().start()

    def z_arrive(t, *onward):
        wgz(t).wait_recv()
        for k in onward:
            cgz(t + k).start()

    def x_send(t):
        for d in range(2):
            cgx(d, away(t)).start()

    def x_relay(t):
        q = away(t)
        for d in range(2):
            wgx(d, q).wait_recv()
            cgh(d, q).start()

    hb = BLOCK // 2

    def outer_send():
        in_g.wait()
        in_m.wait()
        drift = g[...].astype(F32) - w[rowof(x, j), :].astype(F32)
        codes, scales = [], []
        for k in range(KV // BLOCK):
            blk = drift[:, k * BLOCK : (k + 1) * BLOCK]
            scale = (jnp.max(jnp.abs(blk), axis=1, keepdims=True) + scale_epsilon).astype(BF16)
            codes.append((blk / scale.astype(F32)).astype(BF16))
            scales.append(jnp.broadcast_to(scale.astype(F32), (ROWS, hb)).astype(BF16))
        for t in range(NB):
            yy, cc = t // 2, t % 2
            cut = slice(cc * hb, cc * hb + hb)
            oms[t] = jnp.concatenate(
                [codes[yy][:, cut], codes[yy + 4][:, cut], scales[yy], scales[yy + 4]], axis=1
            )
        for o in range(1, NB):
            coa(o).start()

    def outer_sum():
        for o in range(1, NB):
            coa(o).wait_recv()
        mine = oms[b].astype(F32)
        total = mine[:, :BLOCK] * mine[:, BLOCK:]
        for o in range(1, NB):
            got = omr[o].astype(F32)
            total += got[:, :BLOCK] * got[:, BLOCK:]
        ps[0:32] = jnp.concatenate([total[:32], total[32:]], axis=1)
        m = mom[...].T
        ps[32:48] = jnp.concatenate([m[:16], m[16:32], m[32:48], m[48:]], axis=1)
        cpartner().start()

    def outer_update():
        cpartner().wait_recv()
        both = ps[0:32] + pr[0:32]
        mean = jnp.concatenate([both[:, :BLOCK], both[:, BLOCK:]], axis=0) / (2 * NB)
        pm = pr[32:48]
        theirs = jnp.concatenate([pm[:, 0:32], pm[:, 32:64], pm[:, 64:96], pm[:, 96:]], axis=0)
        ours = mom[...].T
        low = zh == 0
        m64 = jnp.concatenate([jnp.where(low, ours, theirs), jnp.where(low, theirs, ours)], axis=1)
        old = jnp.zeros((ROWS, BLOCK), F32)
        for t in range(NB):
            yy, cc = t // 2, t % 2
            lo = yy * BLOCK + cc * hb
            pick = jnp.concatenate([g[:, lo : lo + hb], g[:, 256 + lo : 256 + lo + hb]], axis=1)
            old = jnp.where(b == t, pick.astype(F32), old)
        new_m = outer_momentum * m64 + mean
        share = (old - outer_rate * (mean + outer_momentum * new_m)).astype(BF16)
        nm[...] = jnp.where(low, new_m[:, :hb], new_m[:, hb:]).T
        ngs[...] = jnp.concatenate([share, share], axis=1)
        for o in range(1, NB):
            cog(o).start()

    def outer_collect():
        for o in range(1, NB):
            cog(o).wait_recv()
        ngr[0] = ngs[...]
        for t in range(NB):
            yy, cc = t // 2, t % 2
            lo = yy * BLOCK + cc * hb
            got = ngr[(b - t + NB) % NB]
            ng[:, lo : lo + hb] = got[:, :hb]
            ng[:, 256 + lo : 256 + lo + hb] = got[:, hb:BLOCK]

    def out_column(n, xx):
        cols = pl.ds(pl.multiple_of((xx + NX) % NX * COL, COL), COL)
        return pltpu.make_async_copy(ig.at[:, cols], ig_hbm.at[:, cols], osem.at[n])

    def use_column(n, xx):
        start = pl.multiple_of((xx + NX) % NX * COL, COL)
        wc = w[pl.ds(start, COL), :]
        part = jnp.dot(a[:, pl.ds(start, COL)], wc, preferred_element_type=F32)
        if n == 0:
            kv[...] = part
        elif n < 3:
            kv[...] += part
        else:
            kvb[...] = (kv[...] + part).astype(BF16)
        ig[:, pl.ds(start, COL)] = lax.dot_general(
            ct[...], wc, (((1,), (1,)), ((), ())), preferred_element_type=F32
        ).astype(BF16)
        out_column(n, xx).start()

    outer_send()
    xs[...] = partial_block(x)
    hear1()
    cgz(2).start()
    tell2()
    relay(7)
    relay(6)
    relay(5)
    relay(4)
    hear2(True)
    cgz(4).start()
    relay(3)
    relay(2)
    z_arrive(1)
    z_arrive(2, 1)
    relay(1)
    relay(0)
    x_send(0)
    x_send(1)
    settle(7)
    settle(6)
    x_send(2)
    hear2(False)
    tell4()
    settle(5)
    settle(4)
    z_arrive(4, 2, 1)
    round1(6)
    z_arrive(3)
    x_send(3)
    settle(3)
    settle(2)
    round1(4)
    round1(2)
    hear4()
    outer_sum()
    z_arrive(6, 1)
    x_send(4)
    x_send(6)
    settle(1)
    settle(0)
    round2(4)
    z_arrive(5)
    x_send(5)
    z_arrive(7)
    x_send(7)
    x_relay(0)
    x_relay(1)
    use_column(0, x)
    x_relay(2)
    round1(0)
    round2(0)
    x_relay(3)
    x_relay(4)
    outer_update()
    out_nm = pltpu.make_async_copy(nm, nm_hbm, osem.at[4])
    out_nm.start()
    x_relay(6)
    x_relay(5)
    cz3().wait_recv()
    wg[...] = ((xs[j] + z3r[...]) * (1.0 / (TOK * NX * NZ))).astype(BF16)
    out_wg = pltpu.make_async_copy(wg, wg_hbm, osem.at[5])
    out_wg.start()
    x_relay(7)
    use_column(1, x + 1)
    use_column(2, x - 1)
    outer_collect()
    out_ng = pltpu.make_async_copy(ng, ng_hbm, osem.at[6])
    out_ng.start()
    for t in range(NZ):
        for d in range(2):
            wgh(d, away(t)).wait_recv()
    use_column(3, x + 2)
    out_kv = pltpu.make_async_copy(kvb, kv_hbm, osem.at[7])
    out_kv.start()

    for p in range(NZ):
        for d in range(2):
            c_transit(d, p).wait_send()
            c_own(d, p).wait_send()
            c_sum(d, p).wait_send()
            cgx(d, p).wait_send()
            cgh(d, p).wait_send()
    for t in range(1, NZ):
        cgz(t).wait_send()
    for t in (1, 3, 5, 7):
        cz1(t).wait_send()
    for t in (2, 6):
        cz2(t).wait_send()
    cz3().wait_send()
    for o in range(1, NB):
        coa(o).wait_send()
        cog(o).wait_send()
    cpartner().wait_send()
    for n, xx in enumerate((x, x + 1, x - 1, x + 2)):
        out_column(n, xx).wait()
    for cp in (out_ng, out_nm, out_wg, out_kv):
        cp.wait()


def finish(*refs):
    srcs, dsts, sem = refs[:5], refs[5:10], refs[10]
    copies = [pltpu.make_async_copy(s, d, sem.at[n]) for n, (s, d) in enumerate(zip(srcs, dsts))]
    for cp in copies:
        cp.start()
    for cp in copies:
        cp.wait()


def per_device(local_weights, global_weights, momentum, activations, kv_cotangent):
    dma = pltpu.SemaphoreType.DMA
    hbm = pl.BlockSpec(memory_space=pl.ANY)
    shapes = (
        jax.ShapeDtypeStruct((TOK, KV), BF16),
        jax.ShapeDtypeStruct((TOK, D), BF16),
        jax.ShapeDtypeStruct((ROWS, KV), BF16),
        jax.ShapeDtypeStruct((ROWS, KV), BF16),
        jax.ShapeDtypeStruct((32, ROWS), F32),
    )
    vmem = pltpu.VMEM
    outs = pl.pallas_call(
        kernel,
        name="joined_step",
        out_shape=shapes,
        in_specs=[hbm] * 5,
        out_specs=[hbm] * 5,
        scratch_shapes=[
            vmem((TOK, D), BF16),
            vmem((TOK, KV), BF16),
            vmem((D, KV), BF16),
            vmem((ROWS, KV), BF16),
            vmem((32, ROWS), F32),
            vmem((TOK, KV), F32),
            vmem((TOK, KV), BF16),
            vmem((TOK, D), BF16),
            vmem((ROWS, KV), BF16),
            vmem((ROWS, KV), BF16),
            vmem((32, ROWS), F32),
            vmem((2, NZ, ROWS, KV), BF16),
            vmem((2, NZ, ROWS, KV), BF16),
            vmem((2, NZ, HALF, KV), BF16),
            vmem((2, NZ, HALF, KV), BF16),
            vmem((2, NZ, HALF, KV), F32),
            vmem((NZ, ROWS, KV), F32),
            vmem((4, ROWS, KV), BF16),
            vmem((4, ROWS, KV), BF16),
            vmem((2, ROWS, KV), BF16),
            vmem((2, ROWS, KV), BF16),
            vmem((ROWS, KV), F32),
            vmem((ROWS, KV), F32),
            vmem((NB, ROWS, 128), BF16),
            vmem((NB, ROWS, 128), BF16),
            vmem((48, 128), F32),
            vmem((48, 128), F32),
            vmem((ROWS, 128), BF16),
            vmem((NB, ROWS, 128), BF16),
            dma((5,)),
            dma((8,)),
            pltpu.SemaphoreType.REGULAR((2,)),
            pltpu.SemaphoreType.REGULAR((2,)),
            pltpu.SemaphoreType.REGULAR,
            dma((2, NZ)), dma((2, NZ)),
            dma((2, NZ)), dma((2, NZ)),
            dma((2, NZ)), dma((2, NZ)),
            dma((4,)), dma((4,)),
            dma((2,)), dma((2,)),
            dma(()), dma(()),
            dma((NZ,)), dma((NZ,)),
            dma((2, NZ)), dma((2, NZ)),
            dma((2, NZ)), dma((2, NZ)),
            dma((NB,)), dma((NB,)),
            dma(()), dma(()),
            dma((NB,)), dma((NB,)),
        ],
        compiler_params=pltpu.CompilerParams(
            collective_id=0, has_side_effects=True, vmem_limit_bytes=KERNEL_VMEM
        ),
        cost_estimate=pl.CostEstimate(
            flops=6 * TOK * D * KV, bytes_accessed=6 * 2**20, transcendentals=0
        ),
    )(local_weights[0], global_weights, momentum.T, activations[0], kv_cotangent[0])
    kv, ig, wg, ng, nm = pl.pallas_call(
        finish,
        name="finish",
        out_shape=shapes,
        in_specs=[hbm] * 5,
        out_specs=[hbm] * 5,
        scratch_shapes=[dma((5,))],
        compiler_params=pltpu.CompilerParams(vmem_limit_bytes=2**20),
    )(*outs)
    return kv[None], ig[None], wg[None], ng, nm.T


def solution(mesh):
    placed = (
        P("replica", "fsdp", None),
        P("fsdp", None),
        P("fsdp", "replica"),
        P("replica", "fsdp", None),
        P("replica", "fsdp", None),
    )
    return jax.shard_map(
        per_device,
        mesh=mesh,
        in_specs=placed,
        out_specs=(
            P("replica", "fsdp", None),
            P("replica", "fsdp", None),
            P("replica", "fsdp", None),
            P("fsdp", None),
            P("fsdp", "replica"),
        ),
        check_vma=False,
    )
```

```python
import functools

import jax
import jax.numpy as jnp
from jax import lax
from jax.experimental import pallas as pl
from jax.experimental.pallas import tpu as pltpu
from jax.sharding import PartitionSpec as P

MESH = pl.DeviceIdType.MESH
BLOCK = 64
KERNEL_VMEM = 52 * 2**20
NX = 4
NZ = 8
NB = 8
ROWS = 64
KV = 512
D = 2048
TOK = 256
HALF = ROWS // 2
NLINE = 16
COL = NZ * ROWS

outer_rate = 0.7
outer_momentum = 0.9
scale_epsilon = 1e-06

F32 = jnp.float32
BF16 = jnp.bfloat16


def kernel(
    m_hbm, a_hbm, b_hbm,
    kv_hbm, ig_hbm, wg_hbm, ng_hbm, nm_hbm,
    a, ct, w, g, mom, kv, kvb, ig, wg, ng, nm,
    s1s, s1r, s2s, s2r, keep, xs, z1s, z1r, z2s, z2r, z3s, z3r, oms, omr, ps, pr, ngs, ngr,
    lsem, osem, near, next2, next4,
    tss, trs, oss, ors, s2ss, s2rs, z1ss, z1rs, z2ss, z2rs, z3ss, z3rs,
    gzs, gzr, gxs, gxr, ghs, ghr, oas, oar, pss, prs, ogs, ogr,
):
    r = lax.axis_index("replica")
    f = lax.axis_index("fsdp")
    x = f // NZ
    j = f % NZ
    zh = r // NB
    b = r % NB
    zpos = zh * NZ + j
    bits = (j % 2, j // 2 % 2, j // 4)

    def away(t):
        p = j
        for k in range(3):
            if t >> k & 1:
                p = p + (1 << k) * (1 - 2 * bits[k])
        return p

    def fs(xx, jj):
        return (r, (xx + NX) % NX * NZ + jj)

    def line(zz):
        return (zz // NZ * NB + b, x * NZ + zz % NZ)

    def rowof(xx, q):
        return pl.ds(pl.multiple_of(((xx + NX) % NX * NZ + q) * ROWS, ROWS), ROWS)

    def halfof(xx, q, h):
        return pl.ds(pl.multiple_of(((xx + NX) % NX * NZ + q) * ROWS + h * HALF, HALF), HALF)

    def rcopy(src, dst, ss, rs, device):
        return pltpu.make_async_remote_copy(
            src_ref=src, dst_ref=dst, send_sem=ss, recv_sem=rs, device_id=device, device_id_type=MESH
        )

    def signal(sem, device):
        pl.semaphore_signal(sem, inc=1, device_id=device, device_id_type=MESH)

    barrier = pltpu.get_barrier_semaphore()
    friends = [fs(x + 1, j), fs(x - 1, j)]
    for o in range(1, NB):
        friends.append((zh * NB + (b + o) % NB, f))
    for dev in friends:
        signal(barrier, dev)

    @pl.when(zpos > 0)
    def _():
        signal(barrier, line(zpos - 1))

    @pl.when(zpos < NLINE - 1)
    def _():
        signal(barrier, line(zpos + 1))

    in_a = pltpu.make_async_copy(a_hbm, a, lsem.at[0])
    in_c = pltpu.make_async_copy(b_hbm.at[0:TOK], ct, lsem.at[1])
    in_w = pltpu.make_async_copy(b_hbm.at[TOK : TOK + ROWS], w.at[rowof(x, j)], lsem.at[2])
    in_g = pltpu.make_async_copy(b_hbm.at[TOK + ROWS : TOK + 2 * ROWS], g, lsem.at[3])
    in_m = pltpu.make_async_copy(m_hbm, mom, lsem.at[4])
    for cp in (in_a, in_c, in_w, in_g, in_m):
        cp.start()

    def tell1():
        @pl.when(zpos > 0)
        def _():
            signal(near.at[1], line(zpos - 1))

        @pl.when(zpos < NLINE - 1)
        def _():
            signal(near.at[0], line(zpos + 1))

    def hear1():
        @pl.when(zpos > 0)
        def _():
            pl.semaphore_wait(near.at[0], 1)

        @pl.when(zpos < NLINE - 1)
        def _():
            pl.semaphore_wait(near.at[1], 1)

    def tell2():
        @pl.when(zpos > 1)
        def _():
            signal(next2.at[1], line(zpos - 2))

        @pl.when(zpos < NLINE - 2)
        def _():
            signal(next2.at[0], line(zpos + 2))

    def hear2(inner):
        low = j < NZ // 2 if inner else j >= NZ // 2
        high = j >= NZ // 2 if inner else j < NZ // 2

        @pl.when(high & (zpos > 1))
        def _():
            pl.semaphore_wait(next2.at[0], 1)

        @pl.when(low & (zpos < NLINE - 2))
        def _():
            pl.semaphore_wait(next2.at[1], 1)

    def tell4():
        @pl.when((zpos >= 4) & (zpos < NZ + 4))
        def _():
            signal(next4, line(zpos - 4))

        @pl.when((zpos >= NZ - 4) & (zpos < NLINE - 4))
        def _():
            signal(next4, line(zpos + 4))

    def hear4():
        pl.semaphore_wait(next4, 1)

    def xdev(d):
        return fs(x + 1, j) if d == 0 else fs(x - 1, j)

    top, bottom = slice(0, HALF), slice(HALF, ROWS)

    def c_transit(d, p):
        return rcopy(s1s.at[d, p, top], s1r.at[d, p, top], tss.at[d, p], trs.at[d, p], xdev(d))

    def c_own(d, p):
        return rcopy(s1s.at[d, p, bottom], s1r.at[d, p, bottom], oss.at[d, p], ors.at[d, p], xdev(d))

    def c_sum(d, p):
        return rcopy(s2s.at[d, p], s2r.at[d, p], s2ss.at[d, p], s2rs.at[d, p], xdev(d))

    def cz1(t):
        return rcopy(z1s.at[t // 2], z1r.at[t // 2], z1ss.at[t // 2], z1rs.at[t // 2], fs(x, away(1)))

    def cz2(t):
        return rcopy(z2s.at[t // 4], z2r.at[t // 4], z2ss.at[t // 4], z2rs.at[t // 4], fs(x, away(2)))

    def cz3():
        return rcopy(z3s, z3r, z3ss, z3rs, fs(x, away(4)))

    def cgz(d, q, h):
        rows = halfof(x, q, h)
        return rcopy(
            w.at[rows], w.at[rows], gzs.at[d, h, q], gzr.at[d, h, q], fs(x, j + 1 if d == 0 else j - 1)
        )

    def cgx(d, q):
        return rcopy(w.at[rowof(x, q)], w.at[rowof(x, q)], gxs.at[d, q], gxr.at[d, q], xdev(d))

    def wgx(d, q):
        src = x - 1 if d == 0 else x + 1
        return rcopy(w.at[rowof(src, q)], w.at[rowof(src, q)], gxs.at[d, q], gxr.at[d, q], xdev(d))

    def cgh(d, q):
        src = x - 1 if d == 0 else x + 1
        return rcopy(
            w.at[halfof(src, q, d)], w.at[halfof(src, q, d)], ghs.at[d, q], ghr.at[d, q], xdev(d)
        )

    def wgh(d, q):
        return rcopy(
            w.at[halfof(x + 2, q, d)], w.at[halfof(x + 2, q, d)], ghs.at[d, q], ghr.at[d, q], xdev(d)
        )

    def coa(o):
        to = (b + o) % NB
        return rcopy(oms.at[to], omr.at[o], oas.at[o], oar.at[o], (zh * NB + to, f))

    def cog(o):
        to = (b + o) % NB
        return rcopy(ngs, ngr.at[o], ogs.at[o], ogr.at[o], (zh * NB + to, f))

    def cpartner():
        return rcopy(ps, pr, pss, prs, ((r + NB) % (2 * NB), f))

    def z_forward(k, h):
        @pl.when((j - k >= 0) & (j < NZ - 1))
        def _():
            cgz(0, j - k, h).start()

        @pl.when((j + k < NZ) & (j > 0))
        def _():
            cgz(1, j + k, h).start()

    def partial_block(xx):
        start = pl.multiple_of((xx + NX) % NX * COL, COL)
        return lax.dot_general(
            a[:, pl.ds(start, COL)], ct[...], (((0,), (0,)), ((), ())), preferred_element_type=F32
        ).reshape(NZ, ROWS, KV)

    in_c.wait()
    in_a.wait()
    far = partial_block(x + 2).astype(BF16)
    s1s[0, :, 0:HALF, :] = far[:, :HALF, :]
    s1s[1, :, 0:HALF, :] = far[:, HALF:, :]
    in_w.wait()
    pl.semaphore_wait(barrier, len(friends) + jnp.minimum(zpos, 1) + jnp.minimum(NLINE - 1 - zpos, 1))
    tell1()
    order = (7, 6, 5, 4, 3, 2, 1, 0)
    for t in order:
        for d in range(2):
            c_transit(d, away(t)).start()
    z_forward(0, 0)
    z_forward(0, 1)

    right = partial_block(x + 1)
    s1s[0, :, HALF:, :] = right[:, HALF:, :].astype(BF16)
    keep[0] = right[:, :HALF, :]
    left = partial_block(x - 1)
    s1s[1, :, HALF:, :] = left[:, :HALF, :].astype(BF16)
    keep[1] = left[:, HALF:, :]

    def relay(t):
        p = away(t)
        for d in range(2):
            c_own(d, p).start()
            c_transit(d, p).wait_recv()
            s2s[d, p] = (keep[d, p] + s1r[d, p, top].astype(F32)).astype(BF16)
            c_sum(d, p).start()

    def settle(t):
        p = away(t)
        for d in range(2):
            c_own(d, p).wait_recv()
        for d in range(2):
            c_sum(d, p).wait_recv()
        xs[p, top] += s2r[0, p].astype(F32) + s1r[1, p, bottom].astype(F32)
        xs[p, bottom] += s2r[1, p].astype(F32) + s1r[0, p, bottom].astype(F32)
        if t % 2:
            z1s[t // 2] = xs[p].astype(BF16)
            cz1(t).start()

    def round1(t):
        cz1(t + 1).wait_recv()
        xs[away(t)] += z1r[t // 2].astype(F32)
        if t % 4 == 2:
            z2s[t // 4] = xs[away(t)].astype(BF16)
            cz2(t).start()

    def round2(t):
        cz2(t + 2).wait_recv()
        xs[away(t)] += z2r[t // 4].astype(F32)
        if t == 4:
            z3s[...] = xs[away(t)].astype(BF16)
            cz3().start()

    def z_gather(k):
        for h in range(2):

            @pl.when(j - k >= 0)
            def _():
                cgz(0, j - k, h).wait_recv()

            @pl.when(j + k < NZ)
            def _():
                cgz(1, j + k, h).wait_recv()

            if k < NZ - 1:
                z_forward(k, h)

    def chunk(n):
        m = jnp.minimum(j, NZ - 1 - j)
        near = j - (n + 1) // 2 if n % 2 else j + n // 2
        rest = jnp.where(j < NZ // 2, n, NZ - 1 - n)
        return jnp.where(n <= 2 * m, near, rest)

    def x_send(n):
        for d in range(2):
            cgx(d, chunk(n)).start()

    def x_relay(n):
        q = chunk(n)
        for d in range(2):
            wgx(d, q).wait_recv()
            cgh(d, q).start()

    hb = BLOCK // 2

    def outer_send():
        in_g.wait()
        in_m.wait()
        drift = g[...].astype(F32) - w[rowof(x, j), :].astype(F32)
        codes, scales = [], []
        for k in range(KV // BLOCK):
            blk = drift[:, k * BLOCK : (k + 1) * BLOCK]
            scale = (jnp.max(jnp.abs(blk), axis=1, keepdims=True) + scale_epsilon).astype(BF16)
            codes.append((blk / scale.astype(F32)).astype(BF16))
            scales.append(jnp.broadcast_to(scale.astype(F32), (ROWS, hb)).astype(BF16))
        for t in range(NB):
            yy, cc = t // 2, t % 2
            cut = slice(cc * hb, cc * hb + hb)
            oms[t] = jnp.concatenate(
                [codes[yy][:, cut], codes[yy + 4][:, cut], scales[yy], scales[yy + 4]], axis=1
            )
        for o in range(1, NB):
            coa(o).start()

    def outer_sum():
        for o in range(1, NB):
            coa(o).wait_recv()
        mine = oms[b].astype(F32)
        total = mine[:, :BLOCK] * mine[:, BLOCK:]
        for o in range(1, NB):
            got = omr[o].astype(F32)
            total += got[:, :BLOCK] * got[:, BLOCK:]
        ps[0:32] = jnp.concatenate([total[:32], total[32:]], axis=1)
        m = mom[...].T
        ps[32:48] = jnp.concatenate([m[:16], m[16:32], m[32:48], m[48:]], axis=1)

    def outer_swap(half):
        @pl.when(zh == half)
        def _():
            hear4()
            cpartner().start()

    def outer_update():
        cpartner().wait_recv()
        both = ps[0:32] + pr[0:32]
        mean = jnp.concatenate([both[:, :BLOCK], both[:, BLOCK:]], axis=0) / (2 * NB)
        pm = pr[32:48]
        theirs = jnp.concatenate([pm[:, 0:32], pm[:, 32:64], pm[:, 64:96], pm[:, 96:]], axis=0)
        ours = mom[...].T
        low = zh == 0
        m64 = jnp.concatenate([jnp.where(low, ours, theirs), jnp.where(low, theirs, ours)], axis=1)
        old = jnp.zeros((ROWS, BLOCK), F32)
        for t in range(NB):
            yy, cc = t // 2, t % 2
            lo = yy * BLOCK + cc * hb
            pick = jnp.concatenate([g[:, lo : lo + hb], g[:, 256 + lo : 256 + lo + hb]], axis=1)
            old = jnp.where(b == t, pick.astype(F32), old)
        new_m = outer_momentum * m64 + mean
        share = (old - outer_rate * (mean + outer_momentum * new_m)).astype(BF16)
        nm[...] = jnp.where(low, new_m[:, :hb], new_m[:, hb:]).T
        ngs[...] = jnp.concatenate([share, share], axis=1)
        for o in range(1, NB):
            cog(o).start()

    def outer_collect():
        for o in range(1, NB):
            cog(o).wait_recv()
        ngr[0] = ngs[...]
        for t in range(NB):
            yy, cc = t // 2, t % 2
            lo = yy * BLOCK + cc * hb
            got = ngr[(b - t + NB) % NB]
            ng[:, lo : lo + hb] = got[:, :hb]
            ng[:, 256 + lo : 256 + lo + hb] = got[:, hb:BLOCK]

    def out_column(n, xx):
        cols = pl.ds(pl.multiple_of((xx + NX) % NX * COL, COL), COL)
        return pltpu.make_async_copy(ig.at[:, cols], ig_hbm.at[:, cols], osem.at[n])

    def use_column(n, xx):
        start = pl.multiple_of((xx + NX) % NX * COL, COL)
        wc = w[pl.ds(start, COL), :]
        part = jnp.dot(a[:, pl.ds(start, COL)], wc, preferred_element_type=F32)
        if n == 0:
            kv[...] = part
        elif n < 3:
            kv[...] += part
        else:
            kvb[...] = (kv[...] + part).astype(BF16)
        ig[:, pl.ds(start, COL)] = lax.dot_general(
            ct[...], wc, (((1,), (1,)), ((), ())), preferred_element_type=F32
        ).astype(BF16)
        out_column(n, xx).start()

    outer_send()
    xs[...] = partial_block(x)
    relay(7)
    relay(6)
    relay(5)
    z_gather(1)
    hear1()
    tell2()
    relay(4)
    relay(3)
    relay(2)
    z_gather(2)
    relay(1)
    relay(0)
    outer_sum()
    hear2(True)
    hear2(False)
    tell4()
    outer_swap(1)
    z_gather(3)
    x_send(0)
    x_send(1)
    x_send(2)
    x_send(3)
    settle(7)
    settle(6)
    z_gather(4)
    x_send(4)
    settle(5)
    round1(6)
    settle(4)
    z_gather(5)
    x_send(5)
    settle(3)
    round1(4)
    settle(2)
    z_gather(6)
    x_send(6)
    round2(4)
    settle(1)
    settle(0)
    z_gather(7)
    x_send(7)
    round1(2)
    x_relay(0)
    outer_swap(0)
    x_relay(1)
    round1(0)
    x_relay(2)
    round2(0)
    x_relay(3)
    use_column(0, x)
    x_relay(4)
    x_relay(5)
    x_relay(6)
    x_relay(7)
    use_column(1, x + 1)
    use_column(2, x - 1)
    outer_update()
    out_nm = pltpu.make_async_copy(nm, nm_hbm, osem.at[4])
    out_nm.start()
    cz3().wait_recv()
    wg[...] = ((xs[j] + z3r[...].astype(F32)) * (1.0 / (TOK * NX * NZ))).astype(BF16)
    out_wg = pltpu.make_async_copy(wg, wg_hbm, osem.at[5])
    out_wg.start()
    for t in range(NZ):
        for d in range(2):
            wgh(d, away(t)).wait_recv()
    use_column(3, x + 2)
    out_kv = pltpu.make_async_copy(kvb, kv_hbm, osem.at[7])
    out_kv.start()
    outer_collect()
    out_ng = pltpu.make_async_copy(ng, ng_hbm, osem.at[6])
    out_ng.start()

    for p in range(NZ):
        for d in range(2):
            c_transit(d, p).wait_send()
            c_own(d, p).wait_send()
            c_sum(d, p).wait_send()
            cgx(d, p).wait_send()
            cgh(d, p).wait_send()
    for q in range(NZ):
        @pl.when((q <= j) & (j < NZ - 1))
        def _():
            cgz(0, q, 0).wait_send()
            cgz(0, q, 1).wait_send()

        @pl.when((q >= j) & (j > 0))
        def _():
            cgz(1, q, 0).wait_send()
            cgz(1, q, 1).wait_send()

    for t in (1, 3, 5, 7):
        cz1(t).wait_send()
    for t in (2, 6):
        cz2(t).wait_send()
    cz3().wait_send()
    for o in range(1, NB):
        coa(o).wait_send()
        cog(o).wait_send()
    cpartner().wait_send()
    for n, xx in enumerate((x, x + 1, x - 1, x + 2)):
        out_column(n, xx).wait()
    for cp in (out_ng, out_nm, out_wg, out_kv):
        cp.wait()


def finish(*refs):
    srcs, dsts, sem = refs[:5], refs[5:10], refs[10]
    copies = [pltpu.make_async_copy(s, d, sem.at[n]) for n, (s, d) in enumerate(zip(srcs, dsts))]
    for cp in copies:
        cp.start()
    for cp in copies:
        cp.wait()


def per_device(local_weights, global_weights, momentum, activations, kv_cotangent):
    dma = pltpu.SemaphoreType.DMA
    hbm = pl.BlockSpec(memory_space=pl.ANY)
    shapes = (
        jax.ShapeDtypeStruct((TOK, KV), BF16),
        jax.ShapeDtypeStruct((TOK, D), BF16),
        jax.ShapeDtypeStruct((ROWS, KV), BF16),
        jax.ShapeDtypeStruct((ROWS, KV), BF16),
        jax.ShapeDtypeStruct((32, ROWS), F32),
    )
    vmem = pltpu.VMEM
    bundle = jnp.concatenate([kv_cotangent[0], local_weights[0], global_weights], axis=0)
    outs = pl.pallas_call(
        kernel,
        name="joined_step",
        out_shape=shapes,
        in_specs=[hbm] * 3,
        out_specs=[hbm] * 5,
        scratch_shapes=[
            vmem((TOK, D), BF16),
            vmem((TOK, KV), BF16),
            vmem((D, KV), BF16),
            vmem((ROWS, KV), BF16),
            vmem((32, ROWS), F32),
            vmem((TOK, KV), F32),
            vmem((TOK, KV), BF16),
            vmem((TOK, D), BF16),
            vmem((ROWS, KV), BF16),
            vmem((ROWS, KV), BF16),
            vmem((32, ROWS), F32),
            vmem((2, NZ, ROWS, KV), BF16),
            vmem((2, NZ, ROWS, KV), BF16),
            vmem((2, NZ, HALF, KV), BF16),
            vmem((2, NZ, HALF, KV), BF16),
            vmem((2, NZ, HALF, KV), F32),
            vmem((NZ, ROWS, KV), F32),
            vmem((4, ROWS, KV), BF16),
            vmem((4, ROWS, KV), BF16),
            vmem((2, ROWS, KV), BF16),
            vmem((2, ROWS, KV), BF16),
            vmem((ROWS, KV), BF16),
            vmem((ROWS, KV), BF16),
            vmem((NB, ROWS, 128), BF16),
            vmem((NB, ROWS, 128), BF16),
            vmem((48, 128), F32),
            vmem((48, 128), F32),
            vmem((ROWS, 128), BF16),
            vmem((NB, ROWS, 128), BF16),
            dma((5,)),
            dma((8,)),
            pltpu.SemaphoreType.REGULAR((2,)),
            pltpu.SemaphoreType.REGULAR((2,)),
            pltpu.SemaphoreType.REGULAR,
            dma((2, NZ)), dma((2, NZ)),
            dma((2, NZ)), dma((2, NZ)),
            dma((2, NZ)), dma((2, NZ)),
            dma((4,)), dma((4,)),
            dma((2,)), dma((2,)),
            dma(()), dma(()),
            dma((2, 2, NZ)), dma((2, 2, NZ)),
            dma((2, NZ)), dma((2, NZ)),
            dma((2, NZ)), dma((2, NZ)),
            dma((NB,)), dma((NB,)),
            dma(()), dma(()),
            dma((NB,)), dma((NB,)),
        ],
        compiler_params=pltpu.CompilerParams(
            collective_id=0, has_side_effects=True, vmem_limit_bytes=KERNEL_VMEM
        ),
        cost_estimate=pl.CostEstimate(
            flops=6 * TOK * D * KV, bytes_accessed=6 * 2**20, transcendentals=0
        ),
    )(momentum.T, activations[0], bundle)
    kv, ig, wg, ng, nm = pl.pallas_call(
        finish,
        name="finish",
        out_shape=shapes,
        in_specs=[hbm] * 5,
        out_specs=[hbm] * 5,
        scratch_shapes=[dma((5,))],
        compiler_params=pltpu.CompilerParams(vmem_limit_bytes=2**20),
    )(*outs)
    return kv[None], ig[None], wg[None], ng, nm.T


def solution(mesh):
    placed = (
        P("replica", "fsdp", None),
        P("fsdp", None),
        P("fsdp", "replica"),
        P("replica", "fsdp", None),
        P("replica", "fsdp", None),
    )
    return jax.shard_map(
        per_device,
        mesh=mesh,
        in_specs=placed,
        out_specs=(
            P("replica", "fsdp", None),
            P("replica", "fsdp", None),
            P("replica", "fsdp", None),
            P("fsdp", None),
            P("fsdp", "replica"),
        ),
        check_vma=False,
    )
```

```python
import functools

import jax
import jax.numpy as jnp
from jax import lax
from jax.experimental import pallas as pl
from jax.experimental.pallas import tpu as pltpu
from jax.sharding import PartitionSpec as P

MESH = pl.DeviceIdType.MESH
BLOCK = 64
KERNEL_VMEM = 52 * 2**20
NX = 4
NZ = 8
NB = 8
ROWS = 64
KV = 512
D = 2048
TOK = 256
HALF = ROWS // 2
NLINE = 16
COL = NZ * ROWS

outer_rate = 0.7
outer_momentum = 0.9
scale_epsilon = 1e-06

F32 = jnp.float32
BF16 = jnp.bfloat16


def kernel(
    m_hbm, a_hbm, b_hbm,
    kv_hbm, ig_hbm, wg_hbm, ng_hbm, nm_hbm,
    a, ct, w, g, mom, kv, kvb, ig, wg, ng, nm,
    s1s, s1r, s2s, s2r, keep, xs, z1s, z1r, z2s, z2r, z3s, z3r, oms, omr, ps, pr, ngs, ngr,
    lsem, osem, near, next2, next4,
    tss, trs, oss, ors, s2ss, s2rs, z1ss, z1rs, z2ss, z2rs, z3ss, z3rs,
    gzs, gzr, gxs, gxr, ghs, ghr, oas, oar, pss, prs, ogs, ogr,
):
    r = lax.axis_index("replica")
    f = lax.axis_index("fsdp")
    x = f // NZ
    j = f % NZ
    zh = r // NB
    b = r % NB
    zpos = zh * NZ + j
    bits = (j % 2, j // 2 % 2, j // 4)

    def away(t):
        p = j
        for k in range(3):
            if t >> k & 1:
                p = p + (1 << k) * (1 - 2 * bits[k])
        return p

    def fs(xx, jj):
        return (r, (xx + NX) % NX * NZ + jj)

    def line(zz):
        return (zz // NZ * NB + b, x * NZ + zz % NZ)

    def rowof(xx, q):
        return pl.ds(pl.multiple_of(((xx + NX) % NX * NZ + q) * ROWS, ROWS), ROWS)

    def halfof(xx, q, h):
        return pl.ds(pl.multiple_of(((xx + NX) % NX * NZ + q) * ROWS + h * HALF, HALF), HALF)

    def rcopy(src, dst, ss, rs, device):
        return pltpu.make_async_remote_copy(
            src_ref=src, dst_ref=dst, send_sem=ss, recv_sem=rs, device_id=device, device_id_type=MESH
        )

    def signal(sem, device):
        pl.semaphore_signal(sem, inc=1, device_id=device, device_id_type=MESH)

    barrier = pltpu.get_barrier_semaphore()
    friends = [fs(x + 1, j), fs(x - 1, j)]
    for o in range(1, NB):
        friends.append((zh * NB + (b + o) % NB, f))
    for dev in friends:
        signal(barrier, dev)

    @pl.when(zpos > 0)
    def _():
        signal(barrier, line(zpos - 1))

    @pl.when(zpos < NLINE - 1)
    def _():
        signal(barrier, line(zpos + 1))

    def in_cols(n, xx):
        cols = pl.ds(pl.multiple_of((xx + NX) % NX * COL, COL), COL)
        return pltpu.make_async_copy(a_hbm.at[:, cols], a.at[:, cols], lsem.at[n])

    in_a = [in_cols(n, xx) for n, xx in zip((0, 5, 6, 7), (x + 2, x + 1, x - 1, x))]
    in_c = pltpu.make_async_copy(b_hbm.at[0:TOK], ct, lsem.at[1])
    in_w = pltpu.make_async_copy(b_hbm.at[TOK : TOK + ROWS], w.at[rowof(x, j)], lsem.at[2])
    in_g = pltpu.make_async_copy(b_hbm.at[TOK + ROWS : TOK + 2 * ROWS], g, lsem.at[3])
    in_m = pltpu.make_async_copy(m_hbm, mom, lsem.at[4])
    for cp in (in_w, in_c, *in_a, in_g, in_m):
        cp.start()

    def tell1():
        @pl.when(zpos > 0)
        def _():
            signal(near.at[1], line(zpos - 1))

        @pl.when(zpos < NLINE - 1)
        def _():
            signal(near.at[0], line(zpos + 1))

    def hear1():
        @pl.when(zpos > 0)
        def _():
            pl.semaphore_wait(near.at[0], 1)

        @pl.when(zpos < NLINE - 1)
        def _():
            pl.semaphore_wait(near.at[1], 1)

    def tell2():
        @pl.when(zpos > 1)
        def _():
            signal(next2.at[1], line(zpos - 2))

        @pl.when(zpos < NLINE - 2)
        def _():
            signal(next2.at[0], line(zpos + 2))

    def hear2(inner):
        low = j < NZ // 2 if inner else j >= NZ // 2
        high = j >= NZ // 2 if inner else j < NZ // 2

        @pl.when(high & (zpos > 1))
        def _():
            pl.semaphore_wait(next2.at[0], 1)

        @pl.when(low & (zpos < NLINE - 2))
        def _():
            pl.semaphore_wait(next2.at[1], 1)

    def tell4():
        @pl.when((zpos >= 4) & (zpos < NZ + 4))
        def _():
            signal(next4, line(zpos - 4))

        @pl.when((zpos >= NZ - 4) & (zpos < NLINE - 4))
        def _():
            signal(next4, line(zpos + 4))

    def hear4():
        pl.semaphore_wait(next4, 1)

    def xdev(d):
        return fs(x + 1, j) if d == 0 else fs(x - 1, j)

    top, bottom = slice(0, HALF), slice(HALF, ROWS)

    def c_transit(d, p):
        return rcopy(s1s.at[d, p, top], s1r.at[d, p, top], tss.at[d, p], trs.at[d, p], xdev(d))

    def c_own(d, p):
        return rcopy(s1s.at[d, p, bottom], s1r.at[d, p, bottom], oss.at[d, p], ors.at[d, p], xdev(d))

    def c_sum(d, p):
        return rcopy(s2s.at[d, p], s2r.at[d, p], s2ss.at[d, p], s2rs.at[d, p], xdev(d))

    def cz1(t):
        return rcopy(z1s.at[t // 2], z1r.at[t // 2], z1ss.at[t // 2], z1rs.at[t // 2], fs(x, away(1)))

    def cz2(t):
        return rcopy(z2s.at[t // 4], z2r.at[t // 4], z2ss.at[t // 4], z2rs.at[t // 4], fs(x, away(2)))

    def cz3():
        return rcopy(z3s, z3r, z3ss, z3rs, fs(x, away(4)))

    def cgz(d, q, h):
        rows = halfof(x, q, h)
        return rcopy(
            w.at[rows], w.at[rows], gzs.at[d, h, q], gzr.at[d, h, q], fs(x, j + 1 if d == 0 else j - 1)
        )

    def cgx(d, q):
        return rcopy(w.at[rowof(x, q)], w.at[rowof(x, q)], gxs.at[d, q], gxr.at[d, q], xdev(d))

    def wgx(d, q):
        src = x - 1 if d == 0 else x + 1
        return rcopy(w.at[rowof(src, q)], w.at[rowof(src, q)], gxs.at[d, q], gxr.at[d, q], xdev(d))

    def cgh(d, q):
        src = x - 1 if d == 0 else x + 1
        return rcopy(
            w.at[halfof(src, q, d)], w.at[halfof(src, q, d)], ghs.at[d, q], ghr.at[d, q], xdev(d)
        )

    def wgh(d, q):
        return rcopy(
            w.at[halfof(x + 2, q, d)], w.at[halfof(x + 2, q, d)], ghs.at[d, q], ghr.at[d, q], xdev(d)
        )

    def coa(o):
        to = (b + o) % NB
        return rcopy(oms.at[to], omr.at[o], oas.at[o], oar.at[o], (zh * NB + to, f))

    def cog(o):
        to = (b + o) % NB
        return rcopy(ngs, ngr.at[o], ogs.at[o], ogr.at[o], (zh * NB + to, f))

    def cpartner():
        return rcopy(ps, pr, pss, prs, ((r + NB) % (2 * NB), f))

    def z_forward(k, h):
        @pl.when((j - k >= 0) & (j < NZ - 1))
        def _():
            cgz(0, j - k, h).start()

        @pl.when((j + k < NZ) & (j > 0))
        def _():
            cgz(1, j + k, h).start()

    def partial_block(xx):
        start = pl.multiple_of((xx + NX) % NX * COL, COL)
        return lax.dot_general(
            a[:, pl.ds(start, COL)], ct[...], (((0,), (0,)), ((), ())), preferred_element_type=F32
        ).reshape(NZ, ROWS, KV)

    in_c.wait()
    in_a[0].wait()
    far = partial_block(x + 2).astype(BF16)
    s1s[0, :, 0:HALF, :] = far[:, :HALF, :]
    s1s[1, :, 0:HALF, :] = far[:, HALF:, :]
    in_w.wait()
    pl.semaphore_wait(barrier, len(friends) + jnp.minimum(zpos, 1) + jnp.minimum(NLINE - 1 - zpos, 1))
    tell1()

    def transits(*pieces):
        for t in pieces:
            for d in range(2):
                c_transit(d, away(t)).start()

    transits(7, 6, 5, 4)
    z_forward(0, 0)
    z_forward(0, 1)

    in_a[1].wait()
    right = partial_block(x + 1)
    s1s[0, :, HALF:, :] = right[:, HALF:, :].astype(BF16)
    keep[0] = right[:, :HALF, :]
    in_a[2].wait()
    left = partial_block(x - 1)
    s1s[1, :, HALF:, :] = left[:, :HALF, :].astype(BF16)
    keep[1] = left[:, HALF:, :]

    def relay(t):
        p = away(t)
        for d in range(2):
            c_own(d, p).start()
            c_transit(d, p).wait_recv()
            s2s[d, p] = (keep[d, p] + s1r[d, p, top].astype(F32)).astype(BF16)
            c_sum(d, p).start()

    def settle(t):
        p = away(t)
        for d in range(2):
            c_own(d, p).wait_recv()
        for d in range(2):
            c_sum(d, p).wait_recv()
        xs[p, top] += s2r[0, p].astype(F32) + s1r[1, p, bottom].astype(F32)
        xs[p, bottom] += s2r[1, p].astype(F32) + s1r[0, p, bottom].astype(F32)
        if t % 2:
            z1s[t // 2] = xs[p].astype(BF16)
            cz1(t).start()

    def round1(t):
        cz1(t + 1).wait_recv()
        xs[away(t)] += z1r[t // 2].astype(F32)
        if t % 4 == 2:
            z2s[t // 4] = xs[away(t)].astype(BF16)
            cz2(t).start()

    def round2(t):
        cz2(t + 2).wait_recv()
        xs[away(t)] += z2r[t // 4].astype(F32)
        if t == 4:
            z3s[...] = xs[away(t)].astype(BF16)
            cz3().start()

    def z_gather(k):
        for h in range(2):

            @pl.when(j - k >= 0)
            def _():
                cgz(0, j - k, h).wait_recv()

            @pl.when(j + k < NZ)
            def _():
                cgz(1, j + k, h).wait_recv()

            if k < NZ - 1:
                z_forward(k, h)

    def chunk(n):
        m = jnp.minimum(j, NZ - 1 - j)
        near = j - (n + 1) // 2 if n % 2 else j + n // 2
        rest = jnp.where(j < NZ // 2, n, NZ - 1 - n)
        return jnp.where(n <= 2 * m, near, rest)

    def x_send(n):
        for d in range(2):
            cgx(d, chunk(n)).start()

    def x_relay(n):
        q = chunk(n)
        for d in range(2):
            wgx(d, q).wait_recv()
            cgh(d, q).start()

    hb = BLOCK // 2

    def outer_send():
        in_g.wait()
        in_m.wait()
        drift = g[...].astype(F32) - w[rowof(x, j), :].astype(F32)
        codes, scales = [], []
        for k in range(KV // BLOCK):
            blk = drift[:, k * BLOCK : (k + 1) * BLOCK]
            scale = (jnp.max(jnp.abs(blk), axis=1, keepdims=True) + scale_epsilon).astype(BF16)
            codes.append((blk / scale.astype(F32)).astype(BF16))
            scales.append(jnp.broadcast_to(scale.astype(F32), (ROWS, hb)).astype(BF16))
        for t in range(NB):
            yy, cc = t // 2, t % 2
            cut = slice(cc * hb, cc * hb + hb)
            oms[t] = jnp.concatenate(
                [codes[yy][:, cut], codes[yy + 4][:, cut], scales[yy], scales[yy + 4]], axis=1
            )
        for o in range(1, NB):
            coa(o).start()

    def outer_sum():
        for o in range(1, NB):
            coa(o).wait_recv()
        mine = oms[b].astype(F32)
        total = mine[:, :BLOCK] * mine[:, BLOCK:]
        for o in range(1, NB):
            got = omr[o].astype(F32)
            total += got[:, :BLOCK] * got[:, BLOCK:]
        ps[0:32] = jnp.concatenate([total[:32], total[32:]], axis=1)
        m = mom[...].T
        ps[32:48] = jnp.concatenate([m[:16], m[16:32], m[32:48], m[48:]], axis=1)

    def outer_swap(half):
        @pl.when(zh == half)
        def _():
            hear4()
            cpartner().start()

    def outer_update():
        cpartner().wait_recv()
        both = ps[0:32] + pr[0:32]
        mean = jnp.concatenate([both[:, :BLOCK], both[:, BLOCK:]], axis=0) / (2 * NB)
        pm = pr[32:48]
        theirs = jnp.concatenate([pm[:, 0:32], pm[:, 32:64], pm[:, 64:96], pm[:, 96:]], axis=0)
        ours = mom[...].T
        low = zh == 0
        m64 = jnp.concatenate([jnp.where(low, ours, theirs), jnp.where(low, theirs, ours)], axis=1)
        old = jnp.zeros((ROWS, BLOCK), F32)
        for t in range(NB):
            yy, cc = t // 2, t % 2
            lo = yy * BLOCK + cc * hb
            pick = jnp.concatenate([g[:, lo : lo + hb], g[:, 256 + lo : 256 + lo + hb]], axis=1)
            old = jnp.where(b == t, pick.astype(F32), old)
        new_m = outer_momentum * m64 + mean
        share = (old - outer_rate * (mean + outer_momentum * new_m)).astype(BF16)
        nm[...] = jnp.where(low, new_m[:, :hb], new_m[:, hb:]).T
        ngs[...] = jnp.concatenate([share, share], axis=1)
        for o in range(1, NB):
            cog(o).start()

    def outer_collect():
        for o in range(1, NB):
            cog(o).wait_recv()
        ngr[0] = ngs[...]
        for t in range(NB):
            yy, cc = t // 2, t % 2
            lo = yy * BLOCK + cc * hb
            got = ngr[(b - t + NB) % NB]
            ng[:, lo : lo + hb] = got[:, :hb]
            ng[:, 256 + lo : 256 + lo + hb] = got[:, hb:BLOCK]

    def out_column(n, xx):
        cols = pl.ds(pl.multiple_of((xx + NX) % NX * COL, COL), COL)
        return pltpu.make_async_copy(ig.at[:, cols], ig_hbm.at[:, cols], osem.at[n])

    out_kv = pltpu.make_async_copy(kvb, kv_hbm, osem.at[7])

    def use_column(n, xx):
        start = pl.multiple_of((xx + NX) % NX * COL, COL)
        wc = w[pl.ds(start, COL), :]
        part = jnp.dot(a[:, pl.ds(start, COL)], wc, preferred_element_type=F32)
        if n == 0:
            kv[...] = part
        elif n < 3:
            kv[...] += part
        else:
            kvb[...] = (kv[...] + part).astype(BF16)
            out_kv.start()
        ig[:, pl.ds(start, COL)] = lax.dot_general(
            ct[...], wc, (((1,), (1,)), ((), ())), preferred_element_type=F32
        ).astype(BF16)
        out_column(n, xx).start()

    outer_send()
    in_a[3].wait()
    xs[...] = partial_block(x)
    relay(7)
    relay(6)
    z_gather(1)
    relay(5)
    relay(4)
    transits(3, 2, 1, 0)
    hear1()
    tell2()
    z_gather(2)
    outer_sum()
    settle(7)
    hear2(True)
    hear2(False)
    tell4()
    outer_swap(1)
    settle(6)
    z_gather(3)
    x_send(0)
    settle(5)
    relay(3)
    relay(2)
    relay(1)
    relay(0)
    round1(6)
    settle(4)
    z_gather(4)
    x_send(1)
    x_send(2)
    x_send(3)
    settle(3)
    x_send(4)
    round1(4)
    z_gather(5)
    x_send(5)
    round2(4)
    z_gather(6)
    x_send(6)
    settle(2)
    settle(1)
    round1(2)
    z_gather(7)
    outer_swap(0)
    x_send(7)
    settle(0)
    x_relay(0)
    round1(0)
    x_relay(1)
    round2(0)
    x_relay(2)
    use_column(0, x)
    outer_update()
    out_nm = pltpu.make_async_copy(nm, nm_hbm, osem.at[4])
    out_nm.start()
    x_relay(3)
    x_relay(4)
    x_relay(5)
    x_relay(7)
    x_relay(6)
    use_column(1, x + 1)
    use_column(2, x - 1)
    cz3().wait_recv()
    wg[...] = ((xs[j] + z3r[...].astype(F32)) * (1.0 / (TOK * NX * NZ))).astype(BF16)
    out_wg = pltpu.make_async_copy(wg, wg_hbm, osem.at[5])
    out_wg.start()
    outer_collect()
    out_ng = pltpu.make_async_copy(ng, ng_hbm, osem.at[6])
    out_ng.start()
    for p in range(NZ):
        for d in range(2):
            c_transit(d, p).wait_send()
            c_own(d, p).wait_send()
            c_sum(d, p).wait_send()
            cgx(d, p).wait_send()
    for q in range(NZ):
        @pl.when((q <= j) & (j < NZ - 1))
        def _():
            cgz(0, q, 0).wait_send()
            cgz(0, q, 1).wait_send()

        @pl.when((q >= j) & (j > 0))
        def _():
            cgz(1, q, 0).wait_send()
            cgz(1, q, 1).wait_send()

    for t in (1, 3, 5, 7):
        cz1(t).wait_send()
    for t in (2, 6):
        cz2(t).wait_send()
    cz3().wait_send()
    for o in range(1, NB):
        coa(o).wait_send()
        cog(o).wait_send()
    cpartner().wait_send()
    for t in range(NZ):
        for d in range(2):
            wgh(d, away(t)).wait_recv()
    use_column(3, x + 2)

    for p in range(NZ):
        for d in range(2):
            cgh(d, p).wait_send()
    for n, xx in enumerate((x, x + 1, x - 1, x + 2)):
        out_column(n, xx).wait()
    for cp in (out_ng, out_nm, out_wg, out_kv):
        cp.wait()


def finish(*refs):
    srcs, dsts, sem = refs[:5], refs[5:10], refs[10]
    copies = [pltpu.make_async_copy(s, d, sem.at[n]) for n, (s, d) in enumerate(zip(srcs, dsts))]
    for cp in copies:
        cp.start()
    for cp in copies:
        cp.wait()


def per_device(local_weights, global_weights, momentum, activations, kv_cotangent):
    dma = pltpu.SemaphoreType.DMA
    hbm = pl.BlockSpec(memory_space=pl.ANY)
    shapes = (
        jax.ShapeDtypeStruct((TOK, KV), BF16),
        jax.ShapeDtypeStruct((TOK, D), BF16),
        jax.ShapeDtypeStruct((ROWS, KV), BF16),
        jax.ShapeDtypeStruct((ROWS, KV), BF16),
        jax.ShapeDtypeStruct((32, ROWS), F32),
    )
    vmem = pltpu.VMEM
    bundle = jnp.concatenate([kv_cotangent[0], local_weights[0], global_weights], axis=0)
    outs = pl.pallas_call(
        kernel,
        name="joined_step",
        out_shape=shapes,
        in_specs=[hbm] * 3,
        out_specs=[hbm] * 5,
        scratch_shapes=[
            vmem((TOK, D), BF16),
            vmem((TOK, KV), BF16),
            vmem((D, KV), BF16),
            vmem((ROWS, KV), BF16),
            vmem((32, ROWS), F32),
            vmem((TOK, KV), F32),
            vmem((TOK, KV), BF16),
            vmem((TOK, D), BF16),
            vmem((ROWS, KV), BF16),
            vmem((ROWS, KV), BF16),
            vmem((32, ROWS), F32),
            vmem((2, NZ, ROWS, KV), BF16),
            vmem((2, NZ, ROWS, KV), BF16),
            vmem((2, NZ, HALF, KV), BF16),
            vmem((2, NZ, HALF, KV), BF16),
            vmem((2, NZ, HALF, KV), F32),
            vmem((NZ, ROWS, KV), F32),
            vmem((4, ROWS, KV), BF16),
            vmem((4, ROWS, KV), BF16),
            vmem((2, ROWS, KV), BF16),
            vmem((2, ROWS, KV), BF16),
            vmem((ROWS, KV), BF16),
            vmem((ROWS, KV), BF16),
            vmem((NB, ROWS, 128), BF16),
            vmem((NB, ROWS, 128), BF16),
            vmem((48, 128), F32),
            vmem((48, 128), F32),
            vmem((ROWS, 128), BF16),
            vmem((NB, ROWS, 128), BF16),
            dma((8,)),
            dma((8,)),
            pltpu.SemaphoreType.REGULAR((2,)),
            pltpu.SemaphoreType.REGULAR((2,)),
            pltpu.SemaphoreType.REGULAR,
            dma((2, NZ)), dma((2, NZ)),
            dma((2, NZ)), dma((2, NZ)),
            dma((2, NZ)), dma((2, NZ)),
            dma((4,)), dma((4,)),
            dma((2,)), dma((2,)),
            dma(()), dma(()),
            dma((2, 2, NZ)), dma((2, 2, NZ)),
            dma((2, NZ)), dma((2, NZ)),
            dma((2, NZ)), dma((2, NZ)),
            dma((NB,)), dma((NB,)),
            dma(()), dma(()),
            dma((NB,)), dma((NB,)),
        ],
        compiler_params=pltpu.CompilerParams(
            collective_id=0, has_side_effects=True, vmem_limit_bytes=KERNEL_VMEM
        ),
        cost_estimate=pl.CostEstimate(
            flops=6 * TOK * D * KV, bytes_accessed=6 * 2**20, transcendentals=0
        ),
    )(momentum.T, activations[0], bundle)
    kv, ig, wg, ng, nm = pl.pallas_call(
        finish,
        name="finish",
        out_shape=shapes,
        in_specs=[hbm] * 5,
        out_specs=[hbm] * 5,
        scratch_shapes=[dma((5,))],
        compiler_params=pltpu.CompilerParams(vmem_limit_bytes=2**20),
    )(*outs)
    return kv[None], ig[None], wg[None], ng, nm.T


def solution(mesh):
    placed = (
        P("replica", "fsdp", None),
        P("fsdp", None),
        P("fsdp", "replica"),
        P("replica", "fsdp", None),
        P("replica", "fsdp", None),
    )
    return jax.shard_map(
        per_device,
        mesh=mesh,
        in_specs=placed,
        out_specs=(
            P("replica", "fsdp", None),
            P("replica", "fsdp", None),
            P("replica", "fsdp", None),
            P("fsdp", None),
            P("fsdp", "replica"),
        ),
        check_vma=False,
    )
```

```python
import functools

import jax
import jax.numpy as jnp
from jax import lax
from jax.experimental import pallas as pl
from jax.experimental.pallas import tpu as pltpu
from jax.sharding import PartitionSpec as P

MESH = pl.DeviceIdType.MESH
BLOCK = 64
KERNEL_VMEM = 52 * 2**20
NX = 4
NZ = 8
NB = 8
ROWS = 64
KV = 512
D = 2048
TOK = 256
HALF = ROWS // 2
NLINE = 16
COL = NZ * ROWS

outer_rate = 0.7
outer_momentum = 0.9
scale_epsilon = 1e-06

F32 = jnp.float32
BF16 = jnp.bfloat16


def kernel(
    m_hbm, a_hbm, b_hbm,
    kv_hbm, ig_hbm, wg_hbm, ng_hbm, nm_hbm,
    a, ct, w, g, mom, kv, kvb, ig, wg, ng, nm,
    s1s, s1r, s2s, s2r, keep, xs, z1s, z1r, z2s, z2r, z3s, z3r, oms, omr, ps, pr, ngs, ngr,
    lsem, osem, near, next2, next4,
    tss, trs, oss, ors, s2ss, s2rs, z1ss, z1rs, z2ss, z2rs, z3ss, z3rs,
    gzs, gzr, gxs, gxr, ghs, ghr, oas, oar, pss, prs, ogs, ogr,
):
    r = lax.axis_index("replica")
    f = lax.axis_index("fsdp")
    x = f // NZ
    j = f % NZ
    zh = r // NB
    b = r % NB
    zpos = zh * NZ + j
    bits = (j % 2, j // 2 % 2, j // 4)

    def away(t):
        p = j
        for k in range(3):
            if t >> k & 1:
                p = p + (1 << k) * (1 - 2 * bits[k])
        return p

    def fs(xx, jj):
        return (r, (xx + NX) % NX * NZ + jj)

    def line(zz):
        return (zz // NZ * NB + b, x * NZ + zz % NZ)

    def rowof(xx, q):
        return pl.ds(pl.multiple_of(((xx + NX) % NX * NZ + q) * ROWS, ROWS), ROWS)

    def halfof(xx, q, h):
        return pl.ds(pl.multiple_of(((xx + NX) % NX * NZ + q) * ROWS + h * HALF, HALF), HALF)

    def rcopy(src, dst, ss, rs, device):
        return pltpu.make_async_remote_copy(
            src_ref=src, dst_ref=dst, send_sem=ss, recv_sem=rs, device_id=device, device_id_type=MESH
        )

    def signal(sem, device):
        pl.semaphore_signal(sem, inc=1, device_id=device, device_id_type=MESH)

    barrier = pltpu.get_barrier_semaphore()
    friends = [fs(x + 1, j), fs(x - 1, j)]
    for o in range(1, NB):
        friends.append((zh * NB + (b + o) % NB, f))
    for dev in friends:
        signal(barrier, dev)

    @pl.when(zpos > 0)
    def _():
        signal(barrier, line(zpos - 1))

    @pl.when(zpos < NLINE - 1)
    def _():
        signal(barrier, line(zpos + 1))

    def in_cols(n, xx):
        cols = pl.ds(pl.multiple_of((xx + NX) % NX * COL, COL), COL)
        return pltpu.make_async_copy(a_hbm.at[:, cols], a.at[:, cols], lsem.at[n])

    in_a = [in_cols(n, xx) for n, xx in zip((0, 5, 6, 7), (x + 2, x + 1, x - 1, x))]
    in_c = pltpu.make_async_copy(b_hbm.at[0:TOK], ct, lsem.at[1])
    in_w = pltpu.make_async_copy(b_hbm.at[TOK : TOK + ROWS], w.at[rowof(x, j)], lsem.at[2])
    in_g = pltpu.make_async_copy(b_hbm.at[TOK + ROWS : TOK + 2 * ROWS], g, lsem.at[3])
    in_m = pltpu.make_async_copy(m_hbm, mom, lsem.at[4])
    for cp in (in_w, in_c, *in_a, in_g, in_m):
        cp.start()

    def tell1():
        @pl.when(zpos > 0)
        def _():
            signal(near.at[1], line(zpos - 1))

        @pl.when(zpos < NLINE - 1)
        def _():
            signal(near.at[0], line(zpos + 1))

    def hear1():
        @pl.when(zpos > 0)
        def _():
            pl.semaphore_wait(near.at[0], 1)

        @pl.when(zpos < NLINE - 1)
        def _():
            pl.semaphore_wait(near.at[1], 1)

    def tell2():
        @pl.when(zpos > 1)
        def _():
            signal(next2.at[1], line(zpos - 2))

        @pl.when(zpos < NLINE - 2)
        def _():
            signal(next2.at[0], line(zpos + 2))

    def hear2(inner):
        low = j < NZ // 2 if inner else j >= NZ // 2
        high = j >= NZ // 2 if inner else j < NZ // 2

        @pl.when(high & (zpos > 1))
        def _():
            pl.semaphore_wait(next2.at[0], 1)

        @pl.when(low & (zpos < NLINE - 2))
        def _():
            pl.semaphore_wait(next2.at[1], 1)

    def tell4():
        @pl.when((zpos >= 4) & (zpos < NZ + 4))
        def _():
            signal(next4, line(zpos - 4))

        @pl.when((zpos >= NZ - 4) & (zpos < NLINE - 4))
        def _():
            signal(next4, line(zpos + 4))

    def hear4():
        pl.semaphore_wait(next4, 1)

    def xdev(d):
        return fs(x + 1, j) if d == 0 else fs(x - 1, j)

    top, bottom = slice(0, HALF), slice(HALF, ROWS)

    def c_transit(d, p):
        return rcopy(s1s.at[d, p, top], s1r.at[d, p, top], tss.at[d, p], trs.at[d, p], xdev(d))

    def c_own(d, p):
        return rcopy(s1s.at[d, p, bottom], s1r.at[d, p, bottom], oss.at[d, p], ors.at[d, p], xdev(d))

    def c_sum(d, p):
        return rcopy(s2s.at[d, p], s2r.at[d, p], s2ss.at[d, p], s2rs.at[d, p], xdev(d))

    def cz1(t):
        return rcopy(z1s.at[t // 2], z1r.at[t // 2], z1ss.at[t // 2], z1rs.at[t // 2], fs(x, away(1)))

    def cz2(t):
        return rcopy(z2s.at[t // 4], z2r.at[t // 4], z2ss.at[t // 4], z2rs.at[t // 4], fs(x, away(2)))

    def cz3():
        return rcopy(z3s, z3r, z3ss, z3rs, fs(x, away(4)))

    def cgz(d, q, h):
        rows = halfof(x, q, h)
        return rcopy(
            w.at[rows], w.at[rows], gzs.at[d, h, q], gzr.at[d, h, q], fs(x, j + 1 if d == 0 else j - 1)
        )

    def cgx(d, q):
        return rcopy(w.at[rowof(x, q)], w.at[rowof(x, q)], gxs.at[d, q], gxr.at[d, q], xdev(d))

    def wgx(d, q):
        src = x - 1 if d == 0 else x + 1
        return rcopy(w.at[rowof(src, q)], w.at[rowof(src, q)], gxs.at[d, q], gxr.at[d, q], xdev(d))

    def cgh(d, q):
        src = x - 1 if d == 0 else x + 1
        return rcopy(
            w.at[halfof(src, q, d)], w.at[halfof(src, q, d)], ghs.at[d, q], ghr.at[d, q], xdev(d)
        )

    def wgh(d, q):
        return rcopy(
            w.at[halfof(x + 2, q, d)], w.at[halfof(x + 2, q, d)], ghs.at[d, q], ghr.at[d, q], xdev(d)
        )

    def coa(o):
        to = (b + o) % NB
        return rcopy(oms.at[to], omr.at[o], oas.at[o], oar.at[o], (zh * NB + to, f))

    def cog(o):
        to = (b + o) % NB
        return rcopy(ngs, ngr.at[o], ogs.at[o], ogr.at[o], (zh * NB + to, f))

    def cpartner():
        return rcopy(ps, pr, pss, prs, ((r + NB) % (2 * NB), f))

    def z_forward(k, h):
        @pl.when((j - k >= 0) & (j < NZ - 1))
        def _():
            cgz(0, j - k, h).start()

        @pl.when((j + k < NZ) & (j > 0))
        def _():
            cgz(1, j + k, h).start()

    def partial_block(xx):
        start = pl.multiple_of((xx + NX) % NX * COL, COL)
        return lax.dot_general(
            a[:, pl.ds(start, COL)], ct[...], (((0,), (0,)), ((), ())), preferred_element_type=F32
        ).reshape(NZ, ROWS, KV)

    in_c.wait()
    in_a[0].wait()
    far = partial_block(x + 2).astype(BF16)
    s1s[0, :, 0:HALF, :] = far[:, :HALF, :]
    s1s[1, :, 0:HALF, :] = far[:, HALF:, :]
    in_w.wait()
    pl.semaphore_wait(barrier, len(friends) + jnp.minimum(zpos, 1) + jnp.minimum(NLINE - 1 - zpos, 1))
    tell1()

    def transits(*pieces):
        for t in pieces:
            for d in range(2):
                c_transit(d, away(t)).start()

    transits(7, 6, 5, 4)
    z_forward(0, 0)
    z_forward(0, 1)

    in_a[1].wait()
    right = partial_block(x + 1)
    s1s[0, :, HALF:, :] = right[:, HALF:, :].astype(BF16)
    keep[0] = right[:, :HALF, :]
    in_a[2].wait()
    left = partial_block(x - 1)
    s1s[1, :, HALF:, :] = left[:, :HALF, :].astype(BF16)
    keep[1] = left[:, HALF:, :]

    def relay(t):
        p = away(t)
        for d in range(2):
            c_own(d, p).start()
            c_transit(d, p).wait_recv()
            s2s[d, p] = (keep[d, p] + s1r[d, p, top].astype(F32)).astype(BF16)
            c_sum(d, p).start()

    def settle(t):
        p = away(t)
        for d in range(2):
            c_own(d, p).wait_recv()
        for d in range(2):
            c_sum(d, p).wait_recv()
        xs[p, top] += s2r[0, p].astype(F32) + s1r[1, p, bottom].astype(F32)
        xs[p, bottom] += s2r[1, p].astype(F32) + s1r[0, p, bottom].astype(F32)
        if t % 2:
            z1s[t // 2] = xs[p].astype(BF16)
            cz1(t).start()

    def round1(t):
        cz1(t + 1).wait_recv()
        xs[away(t)] += z1r[t // 2].astype(F32)
        if t % 4 == 2:
            z2s[t // 4] = xs[away(t)].astype(BF16)
            cz2(t).start()

    def round2(t):
        cz2(t + 2).wait_recv()
        xs[away(t)] += z2r[t // 4].astype(F32)
        if t == 4:
            z3s[...] = xs[away(t)].astype(BF16)
            cz3().start()

    def z_gather(k):
        for h in range(2):

            @pl.when(j - k >= 0)
            def _():
                cgz(0, j - k, h).wait_recv()

            @pl.when(j + k < NZ)
            def _():
                cgz(1, j + k, h).wait_recv()

            if k < NZ - 1:
                z_forward(k, h)

    def chunk(n):
        m = jnp.minimum(j, NZ - 1 - j)
        near = j - (n + 1) // 2 if n % 2 else j + n // 2
        rest = jnp.where(j < NZ // 2, n, NZ - 1 - n)
        return jnp.where(n <= 2 * m, near, rest)

    def x_send(n):
        for d in range(2):
            cgx(d, chunk(n)).start()

    def x_relay(n):
        q = chunk(n)
        for d in range(2):
            wgx(d, q).wait_recv()
            cgh(d, q).start()

    hb = BLOCK // 2

    def outer_send():
        in_g.wait()
        in_m.wait()
        drift = g[...].astype(F32) - w[rowof(x, j), :].astype(F32)
        codes, scales = [], []
        for k in range(KV // BLOCK):
            blk = drift[:, k * BLOCK : (k + 1) * BLOCK]
            scale = (jnp.max(jnp.abs(blk), axis=1, keepdims=True) + scale_epsilon).astype(BF16)
            codes.append((blk / scale.astype(F32)).astype(BF16))
            scales.append(jnp.broadcast_to(scale.astype(F32), (ROWS, hb)).astype(BF16))
        for t in range(NB):
            yy, cc = t // 2, t % 2
            cut = slice(cc * hb, cc * hb + hb)
            oms[t] = jnp.concatenate(
                [codes[yy][:, cut], codes[yy + 4][:, cut], scales[yy], scales[yy + 4]], axis=1
            )
        for o in range(1, NB):
            coa(o).start()

    def outer_sum():
        for o in range(1, NB):
            coa(o).wait_recv()
        mine = oms[b].astype(F32)
        total = mine[:, :BLOCK] * mine[:, BLOCK:]
        for o in range(1, NB):
            got = omr[o].astype(F32)
            total += got[:, :BLOCK] * got[:, BLOCK:]
        ps[0:32] = jnp.concatenate([total[:32], total[32:]], axis=1)
        m = mom[...].T
        ps[32:48] = jnp.concatenate([m[:16], m[16:32], m[32:48], m[48:]], axis=1)

    def outer_swap(half):
        @pl.when(zh == half)
        def _():
            hear4()
            cpartner().start()

    def outer_update():
        cpartner().wait_recv()
        both = ps[0:32] + pr[0:32]
        mean = jnp.concatenate([both[:, :BLOCK], both[:, BLOCK:]], axis=0) / (2 * NB)
        pm = pr[32:48]
        theirs = jnp.concatenate([pm[:, 0:32], pm[:, 32:64], pm[:, 64:96], pm[:, 96:]], axis=0)
        ours = mom[...].T
        low = zh == 0
        m64 = jnp.concatenate([jnp.where(low, ours, theirs), jnp.where(low, theirs, ours)], axis=1)
        old = jnp.zeros((ROWS, BLOCK), F32)
        for t in range(NB):
            yy, cc = t // 2, t % 2
            lo = yy * BLOCK + cc * hb
            pick = jnp.concatenate([g[:, lo : lo + hb], g[:, 256 + lo : 256 + lo + hb]], axis=1)
            old = jnp.where(b == t, pick.astype(F32), old)
        new_m = outer_momentum * m64 + mean
        share = (old - outer_rate * (mean + outer_momentum * new_m)).astype(BF16)
        nm[...] = jnp.where(low, new_m[:, :hb], new_m[:, hb:]).T
        ngs[...] = jnp.concatenate([share, share], axis=1)
        for o in range(1, NB):
            cog(o).start()

    def outer_collect():
        for o in range(1, NB):
            cog(o).wait_recv()
        ngr[0] = ngs[...]
        for t in range(NB):
            yy, cc = t // 2, t % 2
            lo = yy * BLOCK + cc * hb
            got = ngr[(b - t + NB) % NB]
            ng[:, lo : lo + hb] = got[:, :hb]
            ng[:, 256 + lo : 256 + lo + hb] = got[:, hb:BLOCK]

    def out_column(n, xx):
        cols = pl.ds(pl.multiple_of((xx + NX) % NX * COL, COL), COL)
        return pltpu.make_async_copy(ig.at[:, cols], ig_hbm.at[:, cols], osem.at[n])

    out_kv = pltpu.make_async_copy(kvb, kv_hbm, osem.at[7])

    def use_column(n, xx):
        start = pl.multiple_of((xx + NX) % NX * COL, COL)
        wc = w[pl.ds(start, COL), :]
        part = jnp.dot(a[:, pl.ds(start, COL)], wc, preferred_element_type=F32)
        if n == 0:
            kv[...] = part
        elif n < 3:
            kv[...] += part
        else:
            kvb[...] = (kv[...] + part).astype(BF16)
            out_kv.start()
        ig[:, pl.ds(start, COL)] = lax.dot_general(
            ct[...], wc, (((1,), (1,)), ((), ())), preferred_element_type=F32
        ).astype(BF16)
        out_column(n, xx).start()

    outer_send()
    in_a[3].wait()
    xs[...] = partial_block(x)
    relay(7)
    relay(6)
    z_gather(1)
    relay(5)
    relay(4)
    transits(3, 2, 1, 0)
    hear1()
    tell2()
    outer_sum()
    z_gather(2)
    settle(7)
    hear2(True)
    hear2(False)
    tell4()
    outer_swap(1)
    settle(6)
    z_gather(3)
    x_send(0)
    settle(5)
    relay(3)
    relay(2)
    relay(1)
    relay(0)
    round1(6)
    settle(4)
    z_gather(4)
    x_send(1)
    x_send(2)
    x_send(3)
    settle(3)
    x_send(4)
    round1(4)
    z_gather(5)
    x_send(5)
    round2(4)
    z_gather(6)
    x_send(6)
    settle(2)
    round1(2)
    settle(1)
    z_gather(7)
    outer_swap(0)
    x_send(7)
    settle(0)
    x_relay(0)
    round1(0)
    x_relay(1)
    round2(0)
    x_relay(2)
    outer_update()
    out_nm = pltpu.make_async_copy(nm, nm_hbm, osem.at[4])
    out_nm.start()
    x_relay(3)
    x_relay(4)
    x_relay(5)
    x_relay(6)
    use_column(0, x)
    x_relay(7)
    use_column(1, x + 1)
    use_column(2, x - 1)
    for p in range(NZ):
        for d in range(2):
            c_transit(d, p).wait_send()
            c_own(d, p).wait_send()
            c_sum(d, p).wait_send()
            cgx(d, p).wait_send()
    for q in range(NZ):
        @pl.when((q <= j) & (j < NZ - 1))
        def _():
            cgz(0, q, 0).wait_send()
            cgz(0, q, 1).wait_send()

        @pl.when((q >= j) & (j > 0))
        def _():
            cgz(1, q, 0).wait_send()
            cgz(1, q, 1).wait_send()

    for t in (1, 3, 5, 7):
        cz1(t).wait_send()
    for t in (2, 6):
        cz2(t).wait_send()
    cz3().wait_send()
    for o in range(1, NB):
        coa(o).wait_send()
        cog(o).wait_send()
    cpartner().wait_send()
    for t in range(NZ):
        for d in range(2):
            wgh(d, away(t)).wait_recv()
    use_column(3, x + 2)
    outer_collect()
    out_ng = pltpu.make_async_copy(ng, ng_hbm, osem.at[6])
    out_ng.start()
    cz3().wait_recv()
    wg[...] = ((xs[j] + z3r[...].astype(F32)) * (1.0 / (TOK * NX * NZ))).astype(BF16)
    out_wg = pltpu.make_async_copy(wg, wg_hbm, osem.at[5])
    out_wg.start()

    for p in range(NZ):
        for d in range(2):
            cgh(d, p).wait_send()
    for n, xx in enumerate((x, x + 1, x - 1, x + 2)):
        out_column(n, xx).wait()
    for cp in (out_ng, out_nm, out_wg, out_kv):
        cp.wait()


def finish(*refs):
    srcs, dsts, sem = refs[:5], refs[5:10], refs[10]
    copies = [pltpu.make_async_copy(s, d, sem.at[n]) for n, (s, d) in enumerate(zip(srcs, dsts))]
    for cp in copies:
        cp.start()
    for cp in copies:
        cp.wait()


def per_device(local_weights, global_weights, momentum, activations, kv_cotangent):
    dma = pltpu.SemaphoreType.DMA
    hbm = pl.BlockSpec(memory_space=pl.ANY)
    shapes = (
        jax.ShapeDtypeStruct((TOK, KV), BF16),
        jax.ShapeDtypeStruct((TOK, D), BF16),
        jax.ShapeDtypeStruct((ROWS, KV), BF16),
        jax.ShapeDtypeStruct((ROWS, KV), BF16),
        jax.ShapeDtypeStruct((32, ROWS), F32),
    )
    vmem = pltpu.VMEM
    bundle = jnp.concatenate([kv_cotangent[0], local_weights[0], global_weights], axis=0)
    outs = pl.pallas_call(
        kernel,
        name="joined_step",
        out_shape=shapes,
        in_specs=[hbm] * 3,
        out_specs=[hbm] * 5,
        scratch_shapes=[
            vmem((TOK, D), BF16),
            vmem((TOK, KV), BF16),
            vmem((D, KV), BF16),
            vmem((ROWS, KV), BF16),
            vmem((32, ROWS), F32),
            vmem((TOK, KV), F32),
            vmem((TOK, KV), BF16),
            vmem((TOK, D), BF16),
            vmem((ROWS, KV), BF16),
            vmem((ROWS, KV), BF16),
            vmem((32, ROWS), F32),
            vmem((2, NZ, ROWS, KV), BF16),
            vmem((2, NZ, ROWS, KV), BF16),
            vmem((2, NZ, HALF, KV), BF16),
            vmem((2, NZ, HALF, KV), BF16),
            vmem((2, NZ, HALF, KV), F32),
            vmem((NZ, ROWS, KV), F32),
            vmem((4, ROWS, KV), BF16),
            vmem((4, ROWS, KV), BF16),
            vmem((2, ROWS, KV), BF16),
            vmem((2, ROWS, KV), BF16),
            vmem((ROWS, KV), BF16),
            vmem((ROWS, KV), BF16),
            vmem((NB, ROWS, 128), BF16),
            vmem((NB, ROWS, 128), BF16),
            vmem((48, 128), F32),
            vmem((48, 128), F32),
            vmem((ROWS, 128), BF16),
            vmem((NB, ROWS, 128), BF16),
            dma((8,)),
            dma((8,)),
            pltpu.SemaphoreType.REGULAR((2,)),
            pltpu.SemaphoreType.REGULAR((2,)),
            pltpu.SemaphoreType.REGULAR,
            dma((2, NZ)), dma((2, NZ)),
            dma((2, NZ)), dma((2, NZ)),
            dma((2, NZ)), dma((2, NZ)),
            dma((4,)), dma((4,)),
            dma((2,)), dma((2,)),
            dma(()), dma(()),
            dma((2, 2, NZ)), dma((2, 2, NZ)),
            dma((2, NZ)), dma((2, NZ)),
            dma((2, NZ)), dma((2, NZ)),
            dma((NB,)), dma((NB,)),
            dma(()), dma(()),
            dma((NB,)), dma((NB,)),
        ],
        compiler_params=pltpu.CompilerParams(
            collective_id=0, has_side_effects=True, vmem_limit_bytes=KERNEL_VMEM
        ),
        cost_estimate=pl.CostEstimate(
            flops=6 * TOK * D * KV, bytes_accessed=6 * 2**20, transcendentals=0
        ),
    )(momentum.T, activations[0], bundle)
    kv, ig, wg, ng, nm = pl.pallas_call(
        finish,
        name="finish",
        out_shape=shapes,
        in_specs=[hbm] * 5,
        out_specs=[hbm] * 5,
        scratch_shapes=[dma((5,))],
        compiler_params=pltpu.CompilerParams(vmem_limit_bytes=2**20),
    )(*outs)
    return kv[None], ig[None], wg[None], ng, nm.T


def solution(mesh):
    placed = (
        P("replica", "fsdp", None),
        P("fsdp", None),
        P("fsdp", "replica"),
        P("replica", "fsdp", None),
        P("replica", "fsdp", None),
    )
    return jax.shard_map(
        per_device,
        mesh=mesh,
        in_specs=placed,
        out_specs=(
            P("replica", "fsdp", None),
            P("replica", "fsdp", None),
            P("replica", "fsdp", None),
            P("fsdp", None),
            P("fsdp", "replica"),
        ),
        check_vma=False,
    )
```

```python
import functools

import jax
import jax.numpy as jnp
from jax import lax
from jax.experimental import pallas as pl
from jax.experimental.pallas import tpu as pltpu
from jax.sharding import PartitionSpec as P

MESH = pl.DeviceIdType.MESH
BLOCK = 64
KERNEL_VMEM = 52 * 2**20
NX = 4
NZ = 8
NB = 8
HUB = 3
ROWS = 64
KV = 512
D = 2048
TOK = 256
HALF = ROWS // 2
NLINE = 16
COL = NZ * ROWS

outer_rate = 0.7
outer_momentum = 0.9
scale_epsilon = 1e-06

F32 = jnp.float32
BF16 = jnp.bfloat16


def kernel(
    m_hbm, a_hbm, b_hbm,
    kv_hbm, ig_hbm, wg_hbm, ng_hbm, nm_hbm,
    a, ct, w, g, mom, kv, kvb, ig, wg, ng, nm,
    s1s, s1r, s2s, s2r, keep, xs, z1s, z1r, z2s, z2r, z3s, z3r, oms, omr, ps, pr, ngs, ngr,
    lsem, osem, ready, near, next2, next4,
    tss, trs, oss, ors, s2ss, s2rs, z1ss, z1rs, z2ss, z2rs, z3ss, z3rs,
    gzs, gzr, gxs, gxr, ghs, ghr, oas, oar, pss, prs, ogs, ogr,
):
    r = lax.axis_index("replica")
    f = lax.axis_index("fsdp")
    x = f // NZ
    j = f % NZ
    zh = r // NB
    b = r % NB
    zpos = zh * NZ + j
    bits = (j % 2, j // 2 % 2, j // 4)

    def away(t):
        p = j
        for k in range(3):
            if t >> k & 1:
                p = p + (1 << k) * (1 - 2 * bits[k])
        return p

    def fs(xx, jj):
        return (r, (xx + NX) % NX * NZ + jj)

    def line(zz):
        return (zz // NZ * NB + b, x * NZ + zz % NZ)

    def rowof(xx, q):
        return pl.ds(pl.multiple_of(((xx + NX) % NX * NZ + q) * ROWS, ROWS), ROWS)

    def halfof(xx, q, h):
        return pl.ds(pl.multiple_of(((xx + NX) % NX * NZ + q) * ROWS + h * HALF, HALF), HALF)

    def rcopy(src, dst, ss, rs, device):
        return pltpu.make_async_remote_copy(
            src_ref=src, dst_ref=dst, send_sem=ss, recv_sem=rs, device_id=device, device_id_type=MESH
        )

    def signal(sem, device):
        pl.semaphore_signal(sem, inc=1, device_id=device, device_id_type=MESH)

    barrier = pltpu.get_barrier_semaphore()
    friends = [fs(x + 1, j), fs(x - 1, j)]
    for dev in friends:
        signal(barrier, dev)

    @pl.when(b == HUB)
    def _():
        for o in range(1, NB):
            signal(barrier, (zh * NB + (HUB + o) % NB, f))

    @pl.when(b != HUB)
    def _():
        signal(barrier, (zh * NB + HUB, f))

    @pl.when(zpos > 0)
    def _():
        signal(barrier, line(zpos - 1))

    @pl.when(zpos < NLINE - 1)
    def _():
        signal(barrier, line(zpos + 1))

    def in_cols(n, xx):
        cols = pl.ds(pl.multiple_of((xx + NX) % NX * COL, COL), COL)
        return pltpu.make_async_copy(a_hbm.at[:, cols], a.at[:, cols], lsem.at[n])

    in_a = [in_cols(n, xx) for n, xx in zip((0, 5, 6, 7), (x + 2, x + 1, x - 1, x))]
    in_c = pltpu.make_async_copy(b_hbm.at[0:TOK], ct, lsem.at[1])
    in_w = pltpu.make_async_copy(b_hbm.at[TOK : TOK + ROWS], w.at[rowof(x, j)], lsem.at[2])
    in_g = pltpu.make_async_copy(b_hbm.at[TOK + ROWS : TOK + 2 * ROWS], g, lsem.at[3])
    in_m = pltpu.make_async_copy(m_hbm, mom, lsem.at[4])
    for cp in (in_w, in_c, *in_a, in_g, in_m):
        cp.start()

    def tell1():
        @pl.when(zpos > 0)
        def _():
            signal(near.at[1], line(zpos - 1))

        @pl.when(zpos < NLINE - 1)
        def _():
            signal(near.at[0], line(zpos + 1))

    def hear1():
        @pl.when(zpos > 0)
        def _():
            pl.semaphore_wait(near.at[0], 1)

        @pl.when(zpos < NLINE - 1)
        def _():
            pl.semaphore_wait(near.at[1], 1)

    def tell2():
        @pl.when(zpos > 1)
        def _():
            signal(next2.at[1], line(zpos - 2))

        @pl.when(zpos < NLINE - 2)
        def _():
            signal(next2.at[0], line(zpos + 2))

    def hear2(inner):
        low = j < NZ // 2 if inner else j >= NZ // 2
        high = j >= NZ // 2 if inner else j < NZ // 2

        @pl.when(high & (zpos > 1))
        def _():
            pl.semaphore_wait(next2.at[0], 1)

        @pl.when(low & (zpos < NLINE - 2))
        def _():
            pl.semaphore_wait(next2.at[1], 1)

    def tell4():
        @pl.when((zpos >= 4) & (zpos < NZ + 4))
        def _():
            signal(next4, line(zpos - 4))

        @pl.when((zpos >= NZ - 4) & (zpos < NLINE - 4))
        def _():
            signal(next4, line(zpos + 4))

    def hear4():
        pl.semaphore_wait(next4, 1)

    def xdev(d):
        return fs(x + 1, j) if d == 0 else fs(x - 1, j)

    top, bottom = slice(0, HALF), slice(HALF, ROWS)

    def c_transit(d, p):
        return rcopy(s1s.at[d, p, top], s1r.at[d, p, top], tss.at[d, p], trs.at[d, p], xdev(d))

    def c_own(d, p):
        return rcopy(s1s.at[d, p, bottom], s1r.at[d, p, bottom], oss.at[d, p], ors.at[d, p], xdev(d))

    def c_sum(d, p):
        return rcopy(s2s.at[d, p], s2r.at[d, p], s2ss.at[d, p], s2rs.at[d, p], xdev(d))

    def cz1(t):
        return rcopy(z1s.at[t // 2], z1r.at[t // 2], z1ss.at[t // 2], z1rs.at[t // 2], fs(x, away(1)))

    def cz2(t):
        return rcopy(z2s.at[t // 4], z2r.at[t // 4], z2ss.at[t // 4], z2rs.at[t // 4], fs(x, away(2)))

    def cz3():
        return rcopy(z3s, z3r, z3ss, z3rs, fs(x, away(4)))

    def cgz(d, q, h):
        rows = halfof(x, q, h)
        return rcopy(
            w.at[rows], w.at[rows], gzs.at[d, h, q], gzr.at[d, h, q], fs(x, (j + (1 if d == 0 else NZ - 1)) % NZ)
        )

    def cgx(d, q):
        return rcopy(w.at[rowof(x, q)], w.at[rowof(x, q)], gxs.at[d, q], gxr.at[d, q], xdev(d))

    def wgx(d, q):
        src = x - 1 if d == 0 else x + 1
        return rcopy(w.at[rowof(src, q)], w.at[rowof(src, q)], gxs.at[d, q], gxr.at[d, q], xdev(d))

    def cgh(d, q):
        src = x - 1 if d == 0 else x + 1
        return rcopy(
            w.at[halfof(src, q, d)], w.at[halfof(src, q, d)], ghs.at[d, q], ghr.at[d, q], xdev(d)
        )

    def wgh(d, q):
        return rcopy(
            w.at[halfof(x + 2, q, d)], w.at[halfof(x + 2, q, d)], ghs.at[d, q], ghr.at[d, q], xdev(d)
        )

    def coa(o):
        to = (b + o) % NB
        return rcopy(oms.at[to], omr.at[o], oas.at[o], oar.at[o], (zh * NB + to, f))

    def cog(o):
        to = (b + o) % NB
        return rcopy(ngs, ngr.at[o], ogs.at[o], ogr.at[o], (zh * NB + to, f))

    def cpartner():
        return rcopy(ps, pr, pss, prs, ((r + NB) % (2 * NB), f))

    def z_forward(k, h):
        @pl.when((j - k >= 0) & (j < NZ - 1))
        def _():
            cgz(0, j - k, h).start()

        @pl.when((j + k < NZ) & (j > 0))
        def _():
            cgz(1, j + k, h).start()

    def partial_block(xx):
        start = pl.multiple_of((xx + NX) % NX * COL, COL)
        return lax.dot_general(
            a[:, pl.ds(start, COL)], ct[...], (((0,), (0,)), ((), ())), preferred_element_type=F32
        ).reshape(NZ, ROWS, KV)

    in_c.wait()
    in_a[0].wait()
    far = partial_block(x + 2).astype(BF16)
    s1s[0, :, 0:HALF, :] = far[:, :HALF, :]
    s1s[1, :, 0:HALF, :] = far[:, HALF:, :]
    in_w.wait()
    sides = jnp.minimum(zpos, 1) + jnp.minimum(NLINE - 1 - zpos, 1)
    pl.semaphore_wait(barrier, len(friends) + sides + jnp.where(b == HUB, NB - 1, 1))

    @pl.when(b == HUB)
    def _():
        for o in range(1, NB):
            signal(ready, (zh * NB + (HUB + o) % NB, f))

    tell1()

    def transits(*pieces):
        for t in pieces:
            for d in range(2):
                c_transit(d, away(t)).start()

    transits(7, 6, 5, 4)
    z_forward(0, 0)
    z_forward(0, 1)

    in_a[1].wait()
    right = partial_block(x + 1)
    s1s[0, :, HALF:, :] = right[:, HALF:, :].astype(BF16)
    keep[0] = right[:, :HALF, :]
    in_a[2].wait()
    left = partial_block(x - 1)
    s1s[1, :, HALF:, :] = left[:, :HALF, :].astype(BF16)
    keep[1] = left[:, HALF:, :]

    def relay(t):
        p = away(t)
        for d in range(2):
            c_own(d, p).start()
            c_transit(d, p).wait_recv()
            s2s[d, p] = (keep[d, p] + s1r[d, p, top].astype(F32)).astype(BF16)
            c_sum(d, p).start()

    def settle(t):
        p = away(t)
        for d in range(2):
            c_own(d, p).wait_recv()
        for d in range(2):
            c_sum(d, p).wait_recv()
        xs[p, top] += s2r[0, p].astype(F32) + s1r[1, p, bottom].astype(F32)
        xs[p, bottom] += s2r[1, p].astype(F32) + s1r[0, p, bottom].astype(F32)
        if t % 2:
            z1s[t // 2] = xs[p].astype(BF16)
            cz1(t).start()

    def round1(t):
        cz1(t + 1).wait_recv()
        xs[away(t)] += z1r[t // 2].astype(F32)
        if t % 4 == 2:
            z2s[t // 4] = xs[away(t)].astype(BF16)
            cz2(t).start()

    def round2(t):
        cz2(t + 2).wait_recv()
        xs[away(t)] += z2r[t // 4].astype(F32)
        if t == 4:
            z3s[...] = xs[away(t)].astype(BF16)
            cz3().start()

    def z_gather(k):
        for h in range(2):

            @pl.when(j - k >= 0)
            def _():
                cgz(0, j - k, h).wait_recv()

            @pl.when(j + k < NZ)
            def _():
                cgz(1, j + k, h).wait_recv()

            if k < NZ - 1:
                z_forward(k, h)

    def chunk(n):
        m = jnp.minimum(j, NZ - 1 - j)
        near = j - (n + 1) // 2 if n % 2 else j + n // 2
        rest = jnp.where(j < NZ // 2, n, NZ - 1 - n)
        return jnp.where(n <= 2 * m, near, rest)

    def x_send(n):
        for d in range(2):
            cgx(d, chunk(n)).start()

    def x_relay(n):
        q = chunk(n)
        for d in range(2):
            wgx(d, q).wait_recv()
            cgh(d, q).start()

    hb = BLOCK // 2

    def outer_codes():
        in_g.wait()
        in_m.wait()
        drift = g[...].astype(F32) - w[rowof(x, j), :].astype(F32)
        codes, scales = [], []
        for k in range(KV // BLOCK):
            blk = drift[:, k * BLOCK : (k + 1) * BLOCK]
            scale = (jnp.max(jnp.abs(blk), axis=1, keepdims=True) + scale_epsilon).astype(BF16)
            codes.append((blk / scale.astype(F32)).astype(BF16))
            scales.append(jnp.broadcast_to(scale.astype(F32), (ROWS, hb)).astype(BF16))
        for t in range(NB):
            yy, cc = t // 2, t % 2
            cut = slice(cc * hb, cc * hb + hb)
            oms[t] = jnp.concatenate(
                [codes[yy][:, cut], codes[yy + 4][:, cut], scales[yy], scales[yy + 4]], axis=1
            )

    def outer_send():
        @pl.when(b != HUB)
        def _():
            pl.semaphore_wait(ready, 1)

        for o in range(1, NB):
            coa(o).start()

    def outer_sum():
        for o in range(1, NB):
            coa(o).wait_recv()
        mine = oms[b].astype(F32)
        total = mine[:, :BLOCK] * mine[:, BLOCK:]
        for o in range(1, NB):
            got = omr[o].astype(F32)
            total += got[:, :BLOCK] * got[:, BLOCK:]
        ps[0:32] = jnp.concatenate([total[:32], total[32:]], axis=1)
        m = mom[...].T
        ps[32:48] = jnp.concatenate([m[:16], m[16:32], m[32:48], m[48:]], axis=1)

    def outer_swap(half):
        @pl.when(zh == half)
        def _():
            hear4()
            cpartner().start()

    def outer_update():
        cpartner().wait_recv()
        both = ps[0:32] + pr[0:32]
        mean = jnp.concatenate([both[:, :BLOCK], both[:, BLOCK:]], axis=0) / (2 * NB)
        pm = pr[32:48]
        theirs = jnp.concatenate([pm[:, 0:32], pm[:, 32:64], pm[:, 64:96], pm[:, 96:]], axis=0)
        ours = mom[...].T
        low = zh == 0
        m64 = jnp.concatenate([jnp.where(low, ours, theirs), jnp.where(low, theirs, ours)], axis=1)
        old = jnp.zeros((ROWS, BLOCK), F32)
        for t in range(NB):
            yy, cc = t // 2, t % 2
            lo = yy * BLOCK + cc * hb
            pick = jnp.concatenate([g[:, lo : lo + hb], g[:, 256 + lo : 256 + lo + hb]], axis=1)
            old = jnp.where(b == t, pick.astype(F32), old)
        new_m = outer_momentum * m64 + mean
        share = (old - outer_rate * (mean + outer_momentum * new_m)).astype(BF16)
        nm[...] = jnp.where(low, new_m[:, :hb], new_m[:, hb:]).T
        ngs[...] = jnp.concatenate([share, share], axis=1)
        for o in range(1, NB):
            cog(o).start()

    def outer_collect():
        for o in range(1, NB):
            cog(o).wait_recv()
        ngr[0] = ngs[...]
        for t in range(NB):
            yy, cc = t // 2, t % 2
            lo = yy * BLOCK + cc * hb
            got = ngr[(b - t + NB) % NB]
            ng[:, lo : lo + hb] = got[:, :hb]
            ng[:, 256 + lo : 256 + lo + hb] = got[:, hb:BLOCK]

    def out_column(n, xx):
        cols = pl.ds(pl.multiple_of((xx + NX) % NX * COL, COL), COL)
        return pltpu.make_async_copy(ig.at[:, cols], ig_hbm.at[:, cols], osem.at[n])

    out_kv = pltpu.make_async_copy(kvb, kv_hbm, osem.at[7])

    def use_column(n, xx):
        start = pl.multiple_of((xx + NX) % NX * COL, COL)
        wc = w[pl.ds(start, COL), :]
        part = jnp.dot(a[:, pl.ds(start, COL)], wc, preferred_element_type=F32)
        if n == 0:
            kv[...] = part
        elif n < 3:
            kv[...] += part
        else:
            kvb[...] = (kv[...] + part).astype(BF16)
            out_kv.start()
        ig[:, pl.ds(start, COL)] = lax.dot_general(
            ct[...], wc, (((1,), (1,)), ((), ())), preferred_element_type=F32
        ).astype(BF16)
        out_column(n, xx).start()

    outer_codes()
    in_a[3].wait()
    xs[...] = partial_block(x)
    relay(7)
    relay(6)
    z_gather(1)
    relay(5)
    relay(4)
    transits(3, 2, 1, 0)
    outer_send()
    hear1()
    tell2()
    z_gather(2)
    settle(7)
    hear2(True)
    hear2(False)
    tell4()
    outer_sum()
    settle(6)
    outer_swap(1)
    z_gather(3)
    x_send(0)
    settle(5)
    relay(3)
    relay(2)
    relay(1)
    relay(0)
    round1(6)
    settle(4)
    z_gather(4)
    x_send(1)
    x_send(2)
    x_send(3)
    settle(3)
    x_send(4)
    round1(4)
    z_gather(5)
    x_send(5)
    round2(4)
    outer_swap(0)
    z_gather(6)
    x_send(6)
    settle(2)
    round1(2)
    settle(1)
    z_gather(7)
    x_send(7)
    settle(0)
    x_relay(0)
    round1(0)
    x_relay(1)
    round2(0)
    x_relay(2)
    outer_update()
    out_nm = pltpu.make_async_copy(nm, nm_hbm, osem.at[4])
    out_nm.start()
    x_relay(3)
    x_relay(4)
    x_relay(5)
    x_relay(6)
    use_column(0, x)
    x_relay(7)
    use_column(1, x + 1)
    use_column(2, x - 1)
    for p in range(NZ):
        for d in range(2):
            c_transit(d, p).wait_send()
            c_own(d, p).wait_send()
            c_sum(d, p).wait_send()
            cgx(d, p).wait_send()
    for q in range(NZ):
        @pl.when((q <= j) & (j < NZ - 1))
        def _():
            cgz(0, q, 0).wait_send()
            cgz(0, q, 1).wait_send()

        @pl.when((q >= j) & (j > 0))
        def _():
            cgz(1, q, 0).wait_send()
            cgz(1, q, 1).wait_send()

    for t in (1, 3, 5, 7):
        cz1(t).wait_send()
    for t in (2, 6):
        cz2(t).wait_send()
    cz3().wait_send()
    for o in range(1, NB):
        coa(o).wait_send()
        cog(o).wait_send()
    cpartner().wait_send()
    for t in range(NZ):
        for d in range(2):
            wgh(d, away(t)).wait_recv()
    use_column(3, x + 2)
    outer_collect()
    out_ng = pltpu.make_async_copy(ng, ng_hbm, osem.at[6])
    out_ng.start()
    cz3().wait_recv()
    wg[...] = ((xs[j] + z3r[...].astype(F32)) * (1.0 / (TOK * NX * NZ))).astype(BF16)
    out_wg = pltpu.make_async_copy(wg, wg_hbm, osem.at[5])
    out_wg.start()

    for p in range(NZ):
        for d in range(2):
            cgh(d, p).wait_send()
    for n, xx in enumerate((x, x + 1, x - 1, x + 2)):
        out_column(n, xx).wait()
    for cp in (out_ng, out_nm, out_wg, out_kv):
        cp.wait()


def finish(*refs):
    srcs, dsts, sem = refs[:5], refs[5:10], refs[10]
    copies = [pltpu.make_async_copy(s, d, sem.at[n]) for n, (s, d) in enumerate(zip(srcs, dsts))]
    for cp in copies:
        cp.start()
    for cp in copies:
        cp.wait()


def per_device(local_weights, global_weights, momentum, activations, kv_cotangent):
    dma = pltpu.SemaphoreType.DMA
    hbm = pl.BlockSpec(memory_space=pl.ANY)
    shapes = (
        jax.ShapeDtypeStruct((TOK, KV), BF16),
        jax.ShapeDtypeStruct((TOK, D), BF16),
        jax.ShapeDtypeStruct((ROWS, KV), BF16),
        jax.ShapeDtypeStruct((ROWS, KV), BF16),
        jax.ShapeDtypeStruct((32, ROWS), F32),
    )
    vmem = pltpu.VMEM
    bundle = jnp.concatenate([kv_cotangent[0], local_weights[0], global_weights], axis=0)
    outs = pl.pallas_call(
        kernel,
        name="joined_step",
        out_shape=shapes,
        in_specs=[hbm] * 3,
        out_specs=[hbm] * 5,
        scratch_shapes=[
            vmem((TOK, D), BF16),
            vmem((TOK, KV), BF16),
            vmem((D, KV), BF16),
            vmem((ROWS, KV), BF16),
            vmem((32, ROWS), F32),
            vmem((TOK, KV), F32),
            vmem((TOK, KV), BF16),
            vmem((TOK, D), BF16),
            vmem((ROWS, KV), BF16),
            vmem((ROWS, KV), BF16),
            vmem((32, ROWS), F32),
            vmem((2, NZ, ROWS, KV), BF16),
            vmem((2, NZ, ROWS, KV), BF16),
            vmem((2, NZ, HALF, KV), BF16),
            vmem((2, NZ, HALF, KV), BF16),
            vmem((2, NZ, HALF, KV), F32),
            vmem((NZ, ROWS, KV), F32),
            vmem((4, ROWS, KV), BF16),
            vmem((4, ROWS, KV), BF16),
            vmem((2, ROWS, KV), BF16),
            vmem((2, ROWS, KV), BF16),
            vmem((ROWS, KV), BF16),
            vmem((ROWS, KV), BF16),
            vmem((NB, ROWS, 128), BF16),
            vmem((NB, ROWS, 128), BF16),
            vmem((48, 128), F32),
            vmem((48, 128), F32),
            vmem((ROWS, 128), BF16),
            vmem((NB, ROWS, 128), BF16),
            dma((8,)),
            dma((8,)),
            pltpu.SemaphoreType.REGULAR,
            pltpu.SemaphoreType.REGULAR((2,)),
            pltpu.SemaphoreType.REGULAR((2,)),
            pltpu.SemaphoreType.REGULAR,
            dma((2, NZ)), dma((2, NZ)),
            dma((2, NZ)), dma((2, NZ)),
            dma((2, NZ)), dma((2, NZ)),
            dma((4,)), dma((4,)),
            dma((2,)), dma((2,)),
            dma(()), dma(()),
            dma((2, 2, NZ)), dma((2, 2, NZ)),
            dma((2, NZ)), dma((2, NZ)),
            dma((2, NZ)), dma((2, NZ)),
            dma((NB,)), dma((NB,)),
            dma(()), dma(()),
            dma((NB,)), dma((NB,)),
        ],
        compiler_params=pltpu.CompilerParams(
            collective_id=0, has_side_effects=True, vmem_limit_bytes=KERNEL_VMEM
        ),
        cost_estimate=pl.CostEstimate(
            flops=6 * TOK * D * KV, bytes_accessed=6 * 2**20, transcendentals=0
        ),
    )(momentum.T, activations[0], bundle)
    kv, ig, wg, ng, nm = pl.pallas_call(
        finish,
        name="finish",
        out_shape=shapes,
        in_specs=[hbm] * 5,
        out_specs=[hbm] * 5,
        scratch_shapes=[dma((5,))],
        compiler_params=pltpu.CompilerParams(vmem_limit_bytes=2**20),
    )(*outs)
    return kv[None], ig[None], wg[None], ng, nm.T


def solution(mesh):
    placed = (
        P("replica", "fsdp", None),
        P("fsdp", None),
        P("fsdp", "replica"),
        P("replica", "fsdp", None),
        P("replica", "fsdp", None),
    )
    return jax.shard_map(
        per_device,
        mesh=mesh,
        in_specs=placed,
        out_specs=(
            P("replica", "fsdp", None),
            P("replica", "fsdp", None),
            P("replica", "fsdp", None),
            P("fsdp", None),
            P("fsdp", "replica"),
        ),
        check_vma=False,
    )
```

```python
import functools

import jax
import jax.numpy as jnp
from jax import lax
from jax.experimental import pallas as pl
from jax.experimental.pallas import tpu as pltpu
from jax.sharding import PartitionSpec as P

MESH = pl.DeviceIdType.MESH
BLOCK = 64
KERNEL_VMEM = 52 * 2**20
NX = 4
NZ = 8
NB = 8
HUB = 7
ROWS = 64
KV = 512
D = 2048
TOK = 256
HALF = ROWS // 2
NLINE = 16
COL = NZ * ROWS

outer_rate = 0.7
outer_momentum = 0.9
scale_epsilon = 1e-06

F32 = jnp.float32
BF16 = jnp.bfloat16


def kernel(
    m_hbm, a_hbm, b_hbm,
    kv_hbm, ig_hbm, wg_hbm, ng_hbm, nm_hbm,
    a, ct, w, g, mom, kv, kvb, ig, wg, ng, nm,
    s1s, s1r, s2s, s2r, keep, xs, z1s, z1r, z2s, z2r, z3s, z3r, oms, omr, ps, pr, ngs, ngr,
    lsem, osem, ready, near, next2, next4,
    tss, trs, oss, ors, s2ss, s2rs, z1ss, z1rs, z2ss, z2rs, z3ss, z3rs,
    gzs, gzr, gxs, gxr, ghs, ghr, oas, oar, pss, prs, ogs, ogr,
):
    r = lax.axis_index("replica")
    f = lax.axis_index("fsdp")
    x = f // NZ
    j = f % NZ
    zh = r // NB
    b = r % NB
    zpos = zh * NZ + j
    bits = (j % 2, j // 2 % 2, j // 4)

    def away(t):
        p = j
        for k in range(3):
            if t >> k & 1:
                p = p + (1 << k) * (1 - 2 * bits[k])
        return p

    def fs(xx, jj):
        return (r, (xx + NX) % NX * NZ + jj)

    def line(zz):
        return (zz // NZ * NB + b, x * NZ + zz % NZ)

    def rowof(xx, q):
        return pl.ds(pl.multiple_of(((xx + NX) % NX * NZ + q) * ROWS, ROWS), ROWS)

    def halfof(xx, q, h):
        return pl.ds(pl.multiple_of(((xx + NX) % NX * NZ + q) * ROWS + h * HALF, HALF), HALF)

    def rcopy(src, dst, ss, rs, device):
        return pltpu.make_async_remote_copy(
            src_ref=src, dst_ref=dst, send_sem=ss, recv_sem=rs, device_id=device, device_id_type=MESH
        )

    def signal(sem, device):
        pl.semaphore_signal(sem, inc=1, device_id=device, device_id_type=MESH)

    barrier = pltpu.get_barrier_semaphore()
    friends = [fs(x + 1, j), fs(x - 1, j)]
    for dev in friends:
        signal(barrier, dev)

    @pl.when(b == HUB)
    def _():
        for o in range(1, NB):
            signal(barrier, (zh * NB + (HUB + o) % NB, f))

    @pl.when(b != HUB)
    def _():
        signal(barrier, (zh * NB + HUB, f))

    @pl.when(zpos > 0)
    def _():
        signal(barrier, line(zpos - 1))

    @pl.when(zpos < NLINE - 1)
    def _():
        signal(barrier, line(zpos + 1))

    def in_cols(n, xx):
        cols = pl.ds(pl.multiple_of((xx + NX) % NX * COL, COL), COL)
        return pltpu.make_async_copy(a_hbm.at[:, cols], a.at[:, cols], lsem.at[n])

    in_a = [in_cols(n, xx) for n, xx in zip((0, 5, 6, 7), (x + 2, x + 1, x - 1, x))]
    in_c = pltpu.make_async_copy(b_hbm.at[0:TOK], ct, lsem.at[1])
    in_w = pltpu.make_async_copy(b_hbm.at[TOK : TOK + ROWS], w.at[rowof(x, j)], lsem.at[2])
    in_g = pltpu.make_async_copy(b_hbm.at[TOK + ROWS : TOK + 2 * ROWS], g, lsem.at[3])
    in_m = pltpu.make_async_copy(m_hbm, mom, lsem.at[4])
    for cp in (in_w, in_c, *in_a, in_g, in_m):
        cp.start()

    def tell1():
        @pl.when(zpos > 0)
        def _():
            signal(near.at[1], line(zpos - 1))

        @pl.when(zpos < NLINE - 1)
        def _():
            signal(near.at[0], line(zpos + 1))

    def hear1():
        @pl.when(zpos > 0)
        def _():
            pl.semaphore_wait(near.at[0], 1)

        @pl.when(zpos < NLINE - 1)
        def _():
            pl.semaphore_wait(near.at[1], 1)

    def tell2():
        @pl.when(zpos > 1)
        def _():
            signal(next2.at[1], line(zpos - 2))

        @pl.when(zpos < NLINE - 2)
        def _():
            signal(next2.at[0], line(zpos + 2))

    def hear2(inner):
        low = j < NZ // 2 if inner else j >= NZ // 2
        high = j >= NZ // 2 if inner else j < NZ // 2

        @pl.when(high & (zpos > 1))
        def _():
            pl.semaphore_wait(next2.at[0], 1)

        @pl.when(low & (zpos < NLINE - 2))
        def _():
            pl.semaphore_wait(next2.at[1], 1)

    def tell4():
        @pl.when((zpos >= 4) & (zpos < NZ + 4))
        def _():
            signal(next4, line(zpos - 4))

        @pl.when((zpos >= NZ - 4) & (zpos < NLINE - 4))
        def _():
            signal(next4, line(zpos + 4))

    def hear4():
        pl.semaphore_wait(next4, 1)

    def xdev(d):
        return fs(x + 1, j) if d == 0 else fs(x - 1, j)

    top, bottom = slice(0, HALF), slice(HALF, ROWS)

    def c_transit(d, p):
        return rcopy(s1s.at[d, p, top], s1r.at[d, p, top], tss.at[d, p], trs.at[d, p], xdev(d))

    def c_own(d, p):
        return rcopy(s1s.at[d, p, bottom], s1r.at[d, p, bottom], oss.at[d, p], ors.at[d, p], xdev(d))

    def c_sum(d, p):
        return rcopy(s2s.at[d, p], s2r.at[d, p], s2ss.at[d, p], s2rs.at[d, p], xdev(d))

    def cz1(t):
        return rcopy(z1s.at[t // 2], z1r.at[t // 2], z1ss.at[t // 2], z1rs.at[t // 2], fs(x, away(1)))

    def cz2(t):
        return rcopy(z2s.at[t // 4], z2r.at[t // 4], z2ss.at[t // 4], z2rs.at[t // 4], fs(x, away(2)))

    def cz3():
        return rcopy(z3s, z3r, z3ss, z3rs, fs(x, away(4)))

    def cgz(d, q, h):
        rows = halfof(x, q, h)
        return rcopy(
            w.at[rows], w.at[rows], gzs.at[d, h, q], gzr.at[d, h, q], fs(x, (j + (1 if d == 0 else NZ - 1)) % NZ)
        )

    def cgx(d, q):
        return rcopy(w.at[rowof(x, q)], w.at[rowof(x, q)], gxs.at[d, q], gxr.at[d, q], xdev(d))

    def wgx(d, q):
        src = x - 1 if d == 0 else x + 1
        return rcopy(w.at[rowof(src, q)], w.at[rowof(src, q)], gxs.at[d, q], gxr.at[d, q], xdev(d))

    def cgh(d, q):
        src = x - 1 if d == 0 else x + 1
        return rcopy(
            w.at[halfof(src, q, d)], w.at[halfof(src, q, d)], ghs.at[d, q], ghr.at[d, q], xdev(d)
        )

    def wgh(d, q):
        return rcopy(
            w.at[halfof(x + 2, q, d)], w.at[halfof(x + 2, q, d)], ghs.at[d, q], ghr.at[d, q], xdev(d)
        )

    def coa(o):
        to = (b + o) % NB
        return rcopy(oms.at[to], omr.at[o], oas.at[o], oar.at[o], (zh * NB + to, f))

    def cog(o):
        to = (b + o) % NB
        return rcopy(ngs, ngr.at[o], ogs.at[o], ogr.at[o], (zh * NB + to, f))

    def cpartner():
        return rcopy(ps, pr, pss, prs, ((r + NB) % (2 * NB), f))

    def z_forward(k, h):
        @pl.when((j - k >= 0) & (j < NZ - 1))
        def _():
            cgz(0, j - k, h).start()

        @pl.when((j + k < NZ) & (j > 0))
        def _():
            cgz(1, j + k, h).start()

    def partial_block(xx):
        start = pl.multiple_of((xx + NX) % NX * COL, COL)
        return lax.dot_general(
            a[:, pl.ds(start, COL)], ct[...], (((0,), (0,)), ((), ())), preferred_element_type=F32
        ).reshape(NZ, ROWS, KV)

    in_c.wait()
    in_a[0].wait()
    far = partial_block(x + 2).astype(BF16)
    s1s[0, :, 0:HALF, :] = far[:, :HALF, :]
    s1s[1, :, 0:HALF, :] = far[:, HALF:, :]
    in_w.wait()
    sides = jnp.minimum(zpos, 1) + jnp.minimum(NLINE - 1 - zpos, 1)
    pl.semaphore_wait(barrier, len(friends) + sides + jnp.where(b == HUB, NB - 1, 1))

    @pl.when(b == HUB)
    def _():
        for o in range(1, NB):
            signal(ready, (zh * NB + (HUB + o) % NB, f))

    tell1()

    def transits(*pieces):
        for t in pieces:
            for d in range(2):
                c_transit(d, away(t)).start()

    transits(7, 6, 5, 4)
    z_forward(0, 0)
    z_forward(0, 1)

    in_a[1].wait()
    right = partial_block(x + 1)
    s1s[0, :, HALF:, :] = right[:, HALF:, :].astype(BF16)
    keep[0] = right[:, :HALF, :]
    in_a[2].wait()
    left = partial_block(x - 1)
    s1s[1, :, HALF:, :] = left[:, :HALF, :].astype(BF16)
    keep[1] = left[:, HALF:, :]

    def relay(t):
        p = away(t)
        for d in range(2):
            c_own(d, p).start()
            c_transit(d, p).wait_recv()
            s2s[d, p] = (keep[d, p] + s1r[d, p, top].astype(F32)).astype(BF16)
            c_sum(d, p).start()

    def settle(t):
        p = away(t)
        for d in range(2):
            c_own(d, p).wait_recv()
        for d in range(2):
            c_sum(d, p).wait_recv()
        xs[p, top] += s2r[0, p].astype(F32) + s1r[1, p, bottom].astype(F32)
        xs[p, bottom] += s2r[1, p].astype(F32) + s1r[0, p, bottom].astype(F32)
        if t % 2:
            z1s[t // 2] = xs[p].astype(BF16)
            cz1(t).start()

    def round1(t):
        cz1(t + 1).wait_recv()
        xs[away(t)] += z1r[t // 2].astype(F32)
        if t % 4 == 2:
            z2s[t // 4] = xs[away(t)].astype(BF16)
            cz2(t).start()

    def round2(t):
        cz2(t + 2).wait_recv()
        xs[away(t)] += z2r[t // 4].astype(F32)
        if t == 4:
            z3s[...] = xs[away(t)].astype(BF16)
            cz3().start()

    def z_gather(k):
        for h in range(2):

            @pl.when(j - k >= 0)
            def _():
                cgz(0, j - k, h).wait_recv()

            @pl.when(j + k < NZ)
            def _():
                cgz(1, j + k, h).wait_recv()

            if k < NZ - 1:
                z_forward(k, h)

    def chunk(n):
        m = jnp.minimum(j, NZ - 1 - j)
        near = j - (n + 1) // 2 if n % 2 else j + n // 2
        rest = jnp.where(j < NZ // 2, n, NZ - 1 - n)
        return jnp.where(n <= 2 * m, near, rest)

    def x_send(n):
        for d in range(2):
            cgx(d, chunk(n)).start()

    def x_relay(n):
        q = chunk(n)
        for d in range(2):
            wgx(d, q).wait_recv()
            cgh(d, q).start()

    hb = BLOCK // 2

    def outer_codes():
        in_g.wait()
        in_m.wait()
        drift = g[...].astype(F32) - w[rowof(x, j), :].astype(F32)
        codes, scales = [], []
        for k in range(KV // BLOCK):
            blk = drift[:, k * BLOCK : (k + 1) * BLOCK]
            scale = (jnp.max(jnp.abs(blk), axis=1, keepdims=True) + scale_epsilon).astype(BF16)
            codes.append((blk / scale.astype(F32)).astype(BF16))
            scales.append(jnp.broadcast_to(scale.astype(F32), (ROWS, hb)).astype(BF16))
        for t in range(NB):
            yy, cc = t // 2, t % 2
            cut = slice(cc * hb, cc * hb + hb)
            oms[t] = jnp.concatenate(
                [codes[yy][:, cut], codes[yy + 4][:, cut], scales[yy], scales[yy + 4]], axis=1
            )

    def outer_send():
        @pl.when(b != HUB)
        def _():
            pl.semaphore_wait(ready, 1)

        for o in range(1, NB):
            coa(o).start()

    def outer_sum():
        for o in range(1, NB):
            coa(o).wait_recv()
        mine = oms[b].astype(F32)
        total = mine[:, :BLOCK] * mine[:, BLOCK:]
        for o in range(1, NB):
            got = omr[o].astype(F32)
            total += got[:, :BLOCK] * got[:, BLOCK:]
        ps[0:32] = jnp.concatenate([total[:32], total[32:]], axis=1)
        m = mom[...].T
        ps[32:48] = jnp.concatenate([m[:16], m[16:32], m[32:48], m[48:]], axis=1)

    def outer_swap(half):
        @pl.when(zh == half)
        def _():
            hear4()
            cpartner().start()

    def outer_update():
        cpartner().wait_recv()
        both = ps[0:32] + pr[0:32]
        mean = jnp.concatenate([both[:, :BLOCK], both[:, BLOCK:]], axis=0) / (2 * NB)
        pm = pr[32:48]
        theirs = jnp.concatenate([pm[:, 0:32], pm[:, 32:64], pm[:, 64:96], pm[:, 96:]], axis=0)
        ours = mom[...].T
        low = zh == 0
        m64 = jnp.concatenate([jnp.where(low, ours, theirs), jnp.where(low, theirs, ours)], axis=1)
        old = jnp.zeros((ROWS, BLOCK), F32)
        for t in range(NB):
            yy, cc = t // 2, t % 2
            lo = yy * BLOCK + cc * hb
            pick = jnp.concatenate([g[:, lo : lo + hb], g[:, 256 + lo : 256 + lo + hb]], axis=1)
            old = jnp.where(b == t, pick.astype(F32), old)
        new_m = outer_momentum * m64 + mean
        share = (old - outer_rate * (mean + outer_momentum * new_m)).astype(BF16)
        nm[...] = jnp.where(low, new_m[:, :hb], new_m[:, hb:]).T
        ngs[...] = jnp.concatenate([share, share], axis=1)
        for o in range(1, NB):
            cog(o).start()

    def outer_collect():
        for o in range(1, NB):
            cog(o).wait_recv()
        ngr[0] = ngs[...]
        for t in range(NB):
            yy, cc = t // 2, t % 2
            lo = yy * BLOCK + cc * hb
            got = ngr[(b - t + NB) % NB]
            ng[:, lo : lo + hb] = got[:, :hb]
            ng[:, 256 + lo : 256 + lo + hb] = got[:, hb:BLOCK]

    def out_column(n, xx):
        cols = pl.ds(pl.multiple_of((xx + NX) % NX * COL, COL), COL)
        return pltpu.make_async_copy(ig.at[:, cols], ig_hbm.at[:, cols], osem.at[n])

    out_kv = pltpu.make_async_copy(kvb, kv_hbm, osem.at[7])

    def use_column(n, xx):
        start = pl.multiple_of((xx + NX) % NX * COL, COL)
        wc = w[pl.ds(start, COL), :]
        part = jnp.dot(a[:, pl.ds(start, COL)], wc, preferred_element_type=F32)
        if n == 0:
            kv[...] = part
        elif n < 3:
            kv[...] += part
        else:
            kvb[...] = (kv[...] + part).astype(BF16)
            out_kv.start()
        ig[:, pl.ds(start, COL)] = lax.dot_general(
            ct[...], wc, (((1,), (1,)), ((), ())), preferred_element_type=F32
        ).astype(BF16)
        out_column(n, xx).start()

    outer_codes()
    in_a[3].wait()
    xs[...] = partial_block(x)
    relay(7)
    relay(6)
    z_gather(1)
    relay(5)
    relay(4)
    transits(3, 2, 1, 0)
    outer_send()
    hear1()
    tell2()
    z_gather(2)
    settle(7)
    hear2(True)
    hear2(False)
    tell4()
    outer_sum()
    settle(6)
    outer_swap(1)
    z_gather(3)
    x_send(0)
    settle(5)
    relay(3)
    relay(2)
    relay(1)
    relay(0)
    round1(6)
    settle(4)
    z_gather(4)
    x_send(1)
    x_send(2)
    x_send(3)
    settle(3)
    x_send(4)
    round1(4)
    z_gather(5)
    x_send(5)
    round2(4)
    outer_swap(0)
    z_gather(6)
    x_send(6)
    settle(2)
    round1(2)
    settle(1)
    z_gather(7)
    x_send(7)
    settle(0)
    x_relay(0)
    round1(0)
    x_relay(1)
    round2(0)
    x_relay(2)
    outer_update()
    out_nm = pltpu.make_async_copy(nm, nm_hbm, osem.at[4])
    out_nm.start()
    x_relay(3)
    x_relay(4)
    x_relay(5)
    x_relay(6)
    use_column(0, x)
    x_relay(7)
    use_column(1, x + 1)
    use_column(2, x - 1)
    for p in range(NZ):
        for d in range(2):
            c_transit(d, p).wait_send()
            c_own(d, p).wait_send()
            c_sum(d, p).wait_send()
            cgx(d, p).wait_send()
    for q in range(NZ):
        @pl.when((q <= j) & (j < NZ - 1))
        def _():
            cgz(0, q, 0).wait_send()
            cgz(0, q, 1).wait_send()

        @pl.when((q >= j) & (j > 0))
        def _():
            cgz(1, q, 0).wait_send()
            cgz(1, q, 1).wait_send()

    for t in (1, 3, 5, 7):
        cz1(t).wait_send()
    for t in (2, 6):
        cz2(t).wait_send()
    cz3().wait_send()
    for o in range(1, NB):
        coa(o).wait_send()
        cog(o).wait_send()
    cpartner().wait_send()
    for t in range(NZ):
        for d in range(2):
            wgh(d, away(t)).wait_recv()
    use_column(3, x + 2)
    outer_collect()
    out_ng = pltpu.make_async_copy(ng, ng_hbm, osem.at[6])
    out_ng.start()
    cz3().wait_recv()
    wg[...] = ((xs[j] + z3r[...].astype(F32)) * (1.0 / (TOK * NX * NZ))).astype(BF16)
    out_wg = pltpu.make_async_copy(wg, wg_hbm, osem.at[5])
    out_wg.start()

    for p in range(NZ):
        for d in range(2):
            cgh(d, p).wait_send()
    for n, xx in enumerate((x, x + 1, x - 1, x + 2)):
        out_column(n, xx).wait()
    for cp in (out_ng, out_nm, out_wg, out_kv):
        cp.wait()


def finish(*refs):
    srcs, dsts, sem = refs[:5], refs[5:10], refs[10]
    copies = [pltpu.make_async_copy(s, d, sem.at[n]) for n, (s, d) in enumerate(zip(srcs, dsts))]
    for cp in copies:
        cp.start()
    for cp in copies:
        cp.wait()


def per_device(local_weights, global_weights, momentum, activations, kv_cotangent):
    dma = pltpu.SemaphoreType.DMA
    hbm = pl.BlockSpec(memory_space=pl.ANY)
    shapes = (
        jax.ShapeDtypeStruct((TOK, KV), BF16),
        jax.ShapeDtypeStruct((TOK, D), BF16),
        jax.ShapeDtypeStruct((ROWS, KV), BF16),
        jax.ShapeDtypeStruct((ROWS, KV), BF16),
        jax.ShapeDtypeStruct((32, ROWS), F32),
    )
    vmem = pltpu.VMEM
    bundle = jnp.concatenate([kv_cotangent[0], local_weights[0], global_weights], axis=0)
    outs = pl.pallas_call(
        kernel,
        name="joined_step",
        out_shape=shapes,
        in_specs=[hbm] * 3,
        out_specs=[hbm] * 5,
        scratch_shapes=[
            vmem((TOK, D), BF16),
            vmem((TOK, KV), BF16),
            vmem((D, KV), BF16),
            vmem((ROWS, KV), BF16),
            vmem((32, ROWS), F32),
            vmem((TOK, KV), F32),
            vmem((TOK, KV), BF16),
            vmem((TOK, D), BF16),
            vmem((ROWS, KV), BF16),
            vmem((ROWS, KV), BF16),
            vmem((32, ROWS), F32),
            vmem((2, NZ, ROWS, KV), BF16),
            vmem((2, NZ, ROWS, KV), BF16),
            vmem((2, NZ, HALF, KV), BF16),
            vmem((2, NZ, HALF, KV), BF16),
            vmem((2, NZ, HALF, KV), F32),
            vmem((NZ, ROWS, KV), F32),
            vmem((4, ROWS, KV), BF16),
            vmem((4, ROWS, KV), BF16),
            vmem((2, ROWS, KV), BF16),
            vmem((2, ROWS, KV), BF16),
            vmem((ROWS, KV), BF16),
            vmem((ROWS, KV), BF16),
            vmem((NB, ROWS, 128), BF16),
            vmem((NB, ROWS, 128), BF16),
            vmem((48, 128), F32),
            vmem((48, 128), F32),
            vmem((ROWS, 128), BF16),
            vmem((NB, ROWS, 128), BF16),
            dma((8,)),
            dma((8,)),
            pltpu.SemaphoreType.REGULAR,
            pltpu.SemaphoreType.REGULAR((2,)),
            pltpu.SemaphoreType.REGULAR((2,)),
            pltpu.SemaphoreType.REGULAR,
            dma((2, NZ)), dma((2, NZ)),
            dma((2, NZ)), dma((2, NZ)),
            dma((2, NZ)), dma((2, NZ)),
            dma((4,)), dma((4,)),
            dma((2,)), dma((2,)),
            dma(()), dma(()),
            dma((2, 2, NZ)), dma((2, 2, NZ)),
            dma((2, NZ)), dma((2, NZ)),
            dma((2, NZ)), dma((2, NZ)),
            dma((NB,)), dma((NB,)),
            dma(()), dma(()),
            dma((NB,)), dma((NB,)),
        ],
        compiler_params=pltpu.CompilerParams(
            collective_id=0, has_side_effects=True, vmem_limit_bytes=KERNEL_VMEM
        ),
        cost_estimate=pl.CostEstimate(
            flops=6 * TOK * D * KV, bytes_accessed=6 * 2**20, transcendentals=0
        ),
    )(momentum.T, activations[0], bundle)
    kv, ig, wg, ng, nm = pl.pallas_call(
        finish,
        name="finish",
        out_shape=shapes,
        in_specs=[hbm] * 5,
        out_specs=[hbm] * 5,
        scratch_shapes=[dma((5,))],
        compiler_params=pltpu.CompilerParams(vmem_limit_bytes=2**20),
    )(*outs)
    return kv[None], ig[None], wg[None], ng, nm.T


def solution(mesh):
    placed = (
        P("replica", "fsdp", None),
        P("fsdp", None),
        P("fsdp", "replica"),
        P("replica", "fsdp", None),
        P("replica", "fsdp", None),
    )
    return jax.shard_map(
        per_device,
        mesh=mesh,
        in_specs=placed,
        out_specs=(
            P("replica", "fsdp", None),
            P("replica", "fsdp", None),
            P("replica", "fsdp", None),
            P("fsdp", None),
            P("fsdp", "replica"),
        ),
        check_vma=False,
    )
```
